512 devices in a mesh: wide: 64 (over z_lo, x, core), narrow: 8 (over z_hi, y).
Axes of the slice: x: 4, y: 4, z: 16 (z_hi: 2, z_lo: 8; z = z_hi * 8 + z_lo), core: 2. Of those that a mesh axis runs over, the one named last changes fastest.
Arguments:
- observations: bfloat16 [2048, 8192], P('narrow', 'wide'), may hold values from -6 to 6
- cotangent: bfloat16 [2048, 8192], P('narrow', 'wide'), may hold values from -0.08984375 to 0.08984375
- cell_basis: bfloat16 [8192, 8192], P(None, 'wide'), may hold values from -0.0625 to 0.0625
- cycle_basis: bfloat16 [2048, 2048], P(None, 'narrow'), may hold values from -0.125 to 0.125
- cell_spectrum: float32 [8192], P('wide'), may hold values from 0.05 to 5
- cycle_spectrum: float32 [2048], P('narrow'), may hold values from 0.1 to 4
- noise_var: float32 [1], replicated, may hold values from 0.3 to 1
Outputs:
- coefficients: bfloat16 [2048, 8192], P('narrow', 'wide')
- basis_grad: float32 [2048, 2048], P('wide', 'narrow')
The draws below stay inside these ranges and needn't reach their ends.
All inputs are finite; a program needn't handle non-finite values.
Results may differ from the reference program's by a relative error of at most 0.0049.
Values may be sent and summed in bfloat16 or wider, within the bound.
A program may use at most 64 MiB of HBM per device.

```python
import math
import jax
import jax.numpy as jnp

N = 8192
M = 2048


def levels(own_key, dims, shards, low, top_value):
    factor_of = 1.0
    for position, shards_of in shards:
        draws = jax.random.uniform(jax.random.fold_in(jax.random.fold_in(own_key, 6), position), (shards_of,), jnp.float32, low / len(shards), top_value / len(shards))
        factor_of = factor_of * jnp.repeat(jnp.exp(draws), dims[position] // shards_of).reshape((-1,) + (1,) * (len(dims) - 1 - position))
    return factor_of


def normal_values(key, dims, deviation, most, shards=(), held_as=jnp.bfloat16):
    gain = levels(key, dims, shards, -0.22, 0.18) if shards else 1.0
    drawn = jax.random.normal(key, dims, jnp.float32) * deviation * gain
    return jnp.minimum(jnp.maximum(drawn, -most), most).astype(held_as)


def setup_inputs(seed: int = 0) -> dict:
    key_of = jax.random.split(jax.random.key(seed), 8)
    observations = normal_values(key_of[0], (M, N), 1.0, 6.0, ((0, 8), (1, 64)))
    cotangent = normal_values(key_of[1], (M, N), 0.015, 0.08984375, ((0, 8), (1, 64)))
    cell_basis = normal_values(key_of[2], (N, N), N ** -0.5, 0.0625, ((1, 64),))
    cycle_basis = normal_values(key_of[3], (M, M), M ** -0.5, 0.125, ((1, 8),))
    cell_spectrum = jnp.clip(jnp.exp(math.log(5.0) - 4.6051702 * jax.random.uniform(key_of[4], (N,), jnp.float32) ** levels(key_of[4], (N,), ((0, 64),), -0.2, 0.2)), 0.05, 5.0)
    cycle_spectrum = jnp.clip(jnp.exp(math.log(4.0) - 3.6888794 * jax.random.uniform(key_of[5], (M,), jnp.float32) ** levels(key_of[5], (M,), ((0, 8),), -0.2, 0.2)), 0.1, 4.0)
    noise_var = jnp.clip(jax.random.uniform(key_of[6], (1,), jnp.float32, 0.3, 1.0), 0.3, 1.0)
    return dict(observations=observations, cotangent=cotangent, cell_basis=cell_basis, cycle_basis=cycle_basis, cell_spectrum=cell_spectrum, cycle_spectrum=cycle_spectrum, noise_var=noise_var)


def reference(observations, cotangent, cell_basis, cycle_basis, cell_spectrum, cycle_spectrum, noise_var):
    proj_data = jnp.dot(observations, cell_basis, preferred_element_type=jnp.float32).astype(jnp.bfloat16)
    proj_cot = jnp.dot(cotangent, cell_basis, preferred_element_type=jnp.float32).astype(jnp.bfloat16)
    rotated = jnp.dot(cycle_basis.T, proj_data, preferred_element_type=jnp.float32)
    rotated_cot = jnp.dot(cycle_basis.T, proj_cot, preferred_element_type=jnp.float32)
    spectrum = cycle_spectrum[:, None] * cell_spectrum[None, :] + noise_var[0]
    coefficients = (rotated / spectrum).astype(jnp.bfloat16)
    scaled_cot = (rotated_cot / spectrum).astype(jnp.bfloat16)
    basis_grad = jnp.dot(proj_cot, coefficients.T, preferred_element_type=jnp.float32)
    basis_grad = basis_grad + jnp.dot(proj_data, scaled_cot.T, preferred_element_type=jnp.float32)
    return coefficients, basis_grad
```

```python
import jax
import jax.numpy as jnp
from jax import lax
from jax.experimental import pallas as pl
from jax.experimental.pallas import tpu as pltpu
from jax.sharding import PartitionSpec as P

F32 = jnp.float32
BF16 = jnp.bfloat16
MESH = pl.DeviceIdType.MESH


def dot_nt(left, right):
    return lax.dot_general(left, right, (((1,), (1,)), ((), ())), preferred_element_type=F32)


def dot_nn(left, right):
    return lax.dot_general(left, right, (((1,), (0,)), ((), ())), preferred_element_type=F32)


def kernel(
    obs, cot, cb, cyc, cell_row, cyc_row, noise,
    coef_out, grad_out,
    G, W, accO, accS, PS, PF, PB, CT, spec, KO, KS, Q, QS, QR, R, RS, RR,
    cb_sem, z_send, z_recv, x1_send, x1_recv, x2_send, x2_recv,
    ps_sem, h_sem, y_send, y_recv, pb_sem, k_sem, qx_send, qx_recv, rz_send, rz_recv,
):
    w = lax.axis_index("wide")
    n = lax.axis_index("narrow")
    l, x, c = w // 8, (w // 2) % 4, w % 2
    h, y = n // 4, n % 4

    def wide(l_, x_, c_):
        return {"wide": (l_ * 4 + x_) * 2 + c_}

    def narrow(h_, y_):
        return {"narrow": h_ * 4 + y_}

    sib = wide(l, x, 1 - c)
    h_peer = narrow(1 - h, y)
    n_peer = (1 - h) * 4 + y
    x_right, x_left = (x + 1) % 4, (x + 3) % 4

    def rcopy(src, dst, ss, rs, dev):
        return pltpu.make_async_remote_copy(
            src_ref=src, dst_ref=dst, send_sem=ss, recv_sem=rs, device_id=dev, device_id_type=MESH
        )

    bar = pltpu.get_barrier_semaphore()

    def greet(dev):
        pl.semaphore_signal(bar, inc=1, device_id=dev, device_id_type=MESH)

    greet(sib)
    greet(h_peer)
    for d in range(1, 4):
        greet(wide(l, (x + d) % 4, c))
        greet(narrow(h, (y + d) % 4))

    @pl.loop(1, 8)
    def _(k):
        greet(wide((l + k) % 8, x, c))

    G[0, l, x] = obs[...]
    G[1, l, x] = cot[...]
    pl.semaphore_wait(bar, 15)

    def z_copy(t, o, up):
        return rcopy(
            G.at[t, o, x], G.at[t, o, x], z_send.at[t, o, up], z_recv.at[t, o],
            wide(l + 2 * up - 1, x, c),
        )

    def x1_copy(t, o, right):
        to = x_right if right else x_left
        return rcopy(
            G.at[t, o, x], G.at[t, o, x], x1_send.at[t, o, right], x1_recv.at[t, o, right],
            wide(l, to, c),
        )

    def x1_wait(t, o, right):
        frm = x_left if right else x_right
        rcopy(
            G.at[t, o, frm], G.at[t, o, frm], x1_send.at[t, o, right], x1_recv.at[t, o, right],
            wide(l, x_right, c),
        ).wait_recv()

    def x2_copy(t, o):
        right = 1 - o % 2
        frm = (x + 1 + 2 * right) % 4
        to = (x + 3 + 2 * right) % 4
        return rcopy(
            G.at[t, o, frm], G.at[t, o, frm], x2_send.at[t, o], x2_recv.at[t, o], wide(l, to, c)
        )

    def x2_wait(t, o):
        far = (x + 2) % 4
        rcopy(
            G.at[t, o, far], G.at[t, o, far], x2_send.at[t, o], x2_recv.at[t, o],
            wide(l, x_right, c),
        ).wait_recv()

    def x1_start(t, o):
        x1_copy(t, o, 1).start()
        x1_copy(t, o, 0).start()

    def z_step(t, k):
        @pl.when(l >= k)
        def _():
            o = l - k
            z_copy(t, o, 1).wait_recv()

            @pl.when(l < 7)
            def _():
                z_copy(t, o, 1).start()

            x1_start(t, o)

        @pl.when(l + k <= 7)
        def _():
            o = l + k
            z_copy(t, o, 1).wait_recv()

            @pl.when(l > 0)
            def _():
                z_copy(t, o, 0).start()

            x1_start(t, o)

    def x2_one(t, o):
        @pl.when(o % 2 == 0)
        def _():
            x1_wait(t, o, 1)

        @pl.when(o % 2 == 1)
        def _():
            x1_wait(t, o, 0)

        x2_copy(t, o).start()

    def mac(t, o):
        @pl.when(o % 2 == 0)
        def _():
            x1_wait(t, o, 0)

        @pl.when(o % 2 == 1)
        def _():
            x1_wait(t, o, 1)

        x2_wait(t, o)
        s = dot_nn(G[t, o, 0], W[o, 0])
        for xx in range(1, 4):
            s = s + dot_nn(G[t, o, xx], W[o, xx])
        accO[t] += s[:, :128]
        accS[t] += s[:, 128:]

    def both(k, f):
        @pl.when(l >= k)
        def _():
            f(l - k)

        @pl.when(l + k <= 7)
        def _():
            f(l + k)

    for t in range(2):
        @pl.when(l < 7)
        def _():
            z_copy(t, l, 1).start()

        @pl.when(l > 0)
        def _():
            z_copy(t, l, 0).start()

        x1_start(t, l)

    def cb_copy():
        return rcopy(
            cb.at[:, :, 1 - c], W.at[:, :, :, pl.ds(128, 128)], cb_sem.at[0], cb_sem.at[1], sib
        )

    cb_copy().start()

    W[:, :, :, :128] = cb[:, :, c]
    accO[...] = jnp.zeros_like(accO)
    accS[...] = jnp.zeros_like(accS)

    @pl.loop(0, 8)
    def _(i):
        CT[i] = cyc[i].T

    spec[...] = (
        jnp.broadcast_to(cyc_row[...], (128, 256)).T * cell_row[...] + noise[0]
    )

    @pl.loop(1, 8)
    def _(k):
        z_step(0, k)

    x2_one(0, l)

    @pl.loop(1, 8)
    def _(k):
        z_step(1, k)
        both(k, lambda o: x2_one(0, o))

    cb_copy().wait_recv()
    x2_one(1, l)
    mac(0, l)

    @pl.loop(1, 8)
    def _(k):
        both(k, lambda o: x2_one(1, o))
        both(k, lambda o: mac(0, o))

    def ps_copy(t):
        return rcopy(accS.at[t], PS.at[t], ps_sem.at[t, 0], ps_sem.at[t, 1], sib)

    def h_copy(t):
        return rcopy(PF.at[t, n], PF.at[t, n], h_sem.at[t, 0], h_sem.at[t, 1], h_peer)

    def h_wait(t):
        rcopy(
            PF.at[t, n_peer], PF.at[t, n_peer], h_sem.at[t, 0], h_sem.at[t, 1], h_peer
        ).wait_recv()

    def y_copy(t, rel, d):
        m = ((h + rel) % 2) * 4 + y
        return rcopy(
            PF.at[t, m], PF.at[t, m], y_send.at[t, rel, d - 1], y_recv.at[t, rel, d - 1],
            narrow(h, (y + d) % 4),
        )

    def y_wait(t, rel, d):
        m = ((h + rel) % 2) * 4 + (y + 4 - d) % 4
        rcopy(
            PF.at[t, m], PF.at[t, m], y_send.at[t, rel, d - 1], y_recv.at[t, rel, d - 1],
            narrow(h, (y + d) % 4),
        ).wait_recv()

    def finish_proj(t):
        ps_copy(t).wait_recv()
        PF[t, n] = (accO[t] + PS[t]).astype(BF16).reshape(4, 2, 32, 128)
        h_copy(t).start()
        for d in (2, 1, 3):
            y_copy(t, 0, d).start()

    def pass_on(t):
        h_wait(t)
        for d in (2, 1, 3):
            y_copy(t, 1, d).start()

    def pb_copy(t):
        return rcopy(PF.at[t, :, :, 1 - c], PB.at[t], pb_sem.at[t, 0], pb_sem.at[t, 1], sib)

    def rotate(t):
        for rel in range(2):
            for d in range(1, 4):
                y_wait(t, rel, d)
        pb_copy(t).start()
        rot = jnp.zeros((256, 128), F32)
        for m in range(8):
            rot = rot + dot_nn(CT[m], PF[t, m].reshape(256, 128))
        KO[t] = (rot / spec[...]).astype(BF16)
        k_copy(t).start()

    def k_copy(t):
        return rcopy(KO.at[t], KS.at[t], k_sem.at[t, 0], k_sem.at[t, 1], sib)

    ps_copy(0).start()
    mac(1, l)
    finish_proj(0)

    @pl.loop(1, 8)
    def _(k):
        both(k, lambda o: mac(1, o))

    ps_copy(1).start()
    pass_on(0)
    finish_proj(1)
    rotate(0)
    coef_out[...] = KO[0]
    pass_on(1)
    rotate(1)

    for t in range(2):
        pb_copy(t).wait_recv()
        k_copy(t).wait_recv()

    def rows(xx):
        q = dot_nt(PF[1, :, xx, c].reshape(256, 128), KO[0])
        q = q + dot_nt(PF[0, :, xx, c].reshape(256, 128), KO[1])
        q = q + dot_nt(PB[1, :, xx].reshape(256, 128), KS[0])
        q = q + dot_nt(PB[0, :, xx].reshape(256, 128), KS[1])
        return q.reshape(8, 32, 256)

    def qx_copy(d):
        return rcopy(
            QS.at[d - 1], QR.at[d - 1], qx_send.at[d - 1], qx_recv.at[d - 1],
            wide(l, (x + d) % 4, c),
        )

    for d in (2, 1, 3):
        QS[d - 1] = rows((x + d) % 4).astype(BF16)
        qx_copy(d).start()
    Q[...] = rows(x)
    for d in (1, 3, 2):
        qx_copy(d).wait_recv()
    R[...] = Q[...] + QR[0].astype(F32) + QR[2].astype(F32) + QR[1].astype(F32)
    RS[...] = R[...].astype(BF16)

    def rz_copy(k):
        to = (l + k) % 8
        return rcopy(RS.at[to], RR.at[l], rz_send.at[k], rz_recv.at[l], wide(to, x, c))

    def rz_wait(k):
        frm = (l + k) % 8
        rcopy(RR.at[frm], RR.at[frm], rz_send.at[k], rz_recv.at[frm], wide(frm, x, c)).wait_recv()

    @pl.loop(1, 8)
    def _(k):
        rz_copy(k).start()

    grad_out[...] = R[l]

    @pl.loop(1, 8)
    def _(k):
        rz_wait(k)
        grad_out[...] += RR[(l + k) % 8].astype(F32)

    cb_copy().wait_send()
    for t in range(2):
        @pl.loop(0, 8)
        def _(o):
            @pl.when(jnp.logical_and(o <= l, l < 7))
            def _():
                z_copy(t, o, 1).wait_send()

            @pl.when(jnp.logical_and(o >= l, l > 0))
            def _():
                z_copy(t, o, 0).wait_send()

            x1_copy(t, o, 1).wait_send()
            x1_copy(t, o, 0).wait_send()
            x2_copy(t, o).wait_send()

        ps_copy(t).wait_send()
        h_copy(t).wait_send()
        for rel in range(2):
            for d in range(1, 4):
                y_copy(t, rel, d).wait_send()
        pb_copy(t).wait_send()
        k_copy(t).wait_send()
    for d in range(1, 4):
        qx_copy(d).wait_send()

    @pl.loop(1, 8)
    def _(k):
        rz_copy(k).wait_send()


def on_device(obs, cot, cell_basis, cycle_basis, cell_spectrum, cycle_spectrum, noise_var):
    vmem = pl.BlockSpec(memory_space=pltpu.VMEM)
    dma = pltpu.SemaphoreType.DMA
    return pl.pallas_call(
        kernel,
        out_shape=(
            jax.ShapeDtypeStruct((256, 128), BF16),
            jax.ShapeDtypeStruct((32, 256), F32),
        ),
        in_specs=[vmem] * 6 + [pl.BlockSpec(memory_space=pltpu.SMEM)],
        out_specs=(vmem, vmem),
        scratch_shapes=[
            pltpu.VMEM((2, 8, 4, 256, 128), BF16),
            pltpu.VMEM((8, 4, 128, 256), BF16),
            pltpu.VMEM((2, 256, 128), F32),
            pltpu.VMEM((2, 256, 128), F32),
            pltpu.VMEM((2, 256, 128), F32),
            pltpu.VMEM((2, 8, 4, 2, 32, 128), BF16),
            pltpu.VMEM((2, 8, 4, 32, 128), BF16),
            pltpu.VMEM((8, 256, 256), BF16),
            pltpu.VMEM((256, 128), F32),
            pltpu.VMEM((2, 256, 128), BF16),
            pltpu.VMEM((2, 256, 128), BF16),
            pltpu.VMEM((8, 32, 256), F32),
            pltpu.VMEM((3, 8, 32, 256), BF16),
            pltpu.VMEM((3, 8, 32, 256), BF16),
            pltpu.VMEM((8, 32, 256), F32),
            pltpu.VMEM((8, 32, 256), BF16),
            pltpu.VMEM((8, 32, 256), BF16),
            dma((2,)),
            dma((2, 8, 2)), dma((2, 8)),
            dma((2, 8, 2)), dma((2, 8, 2)),
            dma((2, 8)), dma((2, 8)),
            dma((2, 2)), dma((2, 2)),
            dma((2, 2, 3)), dma((2, 2, 3)),
            dma((2, 2)), dma((2, 2)),
            dma((3,)), dma((3,)),
            dma((8,)), dma((8,)),
        ],
        compiler_params=pltpu.CompilerParams(
            collective_id=0, has_side_effects=True, vmem_limit_bytes=48 << 20
        ),
    )(
        obs,
        cot,
        cell_basis.reshape(8, 4, 2, 128, 128),
        cycle_basis.reshape(8, 256, 256),
        cell_spectrum.reshape(1, 128),
        cycle_spectrum.reshape(1, 256),
        noise_var,
    )


def solution(mesh):
    in_specs = (
        P("narrow", "wide"),
        P("narrow", "wide"),
        P(None, "wide"),
        P(None, "narrow"),
        P("wide"),
        P("narrow"),
        P(),
    )
    out_specs = (P("narrow", "wide"), P("wide", "narrow"))
    return jax.shard_map(
        on_device, mesh=mesh, in_specs=in_specs, out_specs=out_specs, check_vma=False
    )
```

```python
import jax
import jax.numpy as jnp
from jax import lax
from jax.experimental import pallas as pl
from jax.experimental.pallas import tpu as pltpu
from jax.sharding import PartitionSpec as P

F32 = jnp.float32
BF16 = jnp.bfloat16
MESH = pl.DeviceIdType.MESH


def dot_nt(left, right):
    return lax.dot_general(left, right, (((1,), (1,)), ((), ())), preferred_element_type=F32)


def dot_nn(left, right):
    return lax.dot_general(left, right, (((1,), (0,)), ((), ())), preferred_element_type=F32)


def kernel(
    obs, cot, cb, cyc, cell_row, cyc_row, noise,
    coef_out, grad_out,
    G, W, acc, XS, XR, PF, PB, cycV, CT, cellV, cycrV, noiseV, spec, KO, KS,
    Q, QS, QR, R, RS, RR,
    in_sem, z_send, zj_send, z_recv, g_send, g_recv,
    wx_send, wx_recv, wy_send, wy_recv, xr_send, xr_recv,
    h_sem, y_send, y_recv, pb_sem, k_sem, qx_send, qx_recv, rz_send, rz_recv,
):
    w = lax.axis_index("wide")
    n = lax.axis_index("narrow")
    l, x, c = w // 8, (w // 2) % 4, w % 2
    h, y = n // 4, n % 4

    def wide(l_, x_, c_):
        return {"wide": (l_ * 4 + x_) * 2 + c_}

    def narrow(h_, y_):
        return {"narrow": h_ * 4 + y_}

    sib = wide(l, x, 1 - c)
    h_peer = narrow(1 - h, y)
    n_peer = (1 - h) * 4 + y

    def rcopy(src, dst, ss, rs, dev):
        return pltpu.make_async_remote_copy(
            src_ref=src, dst_ref=dst, send_sem=ss, recv_sem=rs, device_id=dev, device_id_type=MESH
        )

    bar = pltpu.get_barrier_semaphore()

    def greet(dev):
        pl.semaphore_signal(bar, inc=1, device_id=dev, device_id_type=MESH)

    greet(h_peer)

    @pl.loop(1, 8)
    def _(k):
        greet(wide((l + k) % 8, x, c))

    for d in range(1, 4):
        greet(wide(l, (x + d) % 4, c))
        greet(narrow(h, (y + d) % 4))
    greet(sib)

    loads = [
        pltpu.make_async_copy(obs, G.at[0, l, c], in_sem.at[0]),
        pltpu.make_async_copy(cot, G.at[1, l, c], in_sem.at[1]),
        pltpu.make_async_copy(cb.at[:, x], W.at[:, :, :, pl.ds(0, 128)], in_sem.at[2]),
        pltpu.make_async_copy(cyc, cycV, in_sem.at[3]),
        pltpu.make_async_copy(cell_row, cellV, in_sem.at[4]),
        pltpu.make_async_copy(cyc_row, cycrV, in_sem.at[5]),
        pltpu.make_async_copy(noise, noiseV, in_sem.at[6]),
    ]
    for load in loads:
        load.start()
    loads[0].wait()
    loads[1].wait()
    pl.semaphore_wait(bar, 15)

    def z_copy(t, o, up):
        return rcopy(
            G.at[t, o, c], G.at[t, o, c], z_send.at[t, o, up], z_recv.at[t, o],
            wide(l + 2 * up - 1, x, c),
        )

    def z_jump(t, up):
        return rcopy(
            G.at[t, l, c], G.at[t, l, c], zj_send.at[t, up], z_recv.at[t, l],
            wide(l + 8 * up - 4, x, c),
        )

    def g_copy(t, o):
        return rcopy(G.at[t, o, c], G.at[t, o, c], g_send.at[t, o], g_recv.at[t, o], sib)

    def g_wait(t, o):
        rcopy(
            G.at[t, o, 1 - c], G.at[t, o, 1 - c], g_send.at[t, o], g_recv.at[t, o], sib
        ).wait_recv()

    def z_step(t, k):
        @pl.when(l >= k)
        def _():
            o = l - k
            z_copy(t, o, 1).wait_recv()
            if k != 3:
                @pl.when(l < 7)
                def _():
                    z_copy(t, o, 1).start()

            g_copy(t, o).start()

        @pl.when(l + k <= 7)
        def _():
            o = l + k
            z_copy(t, o, 1).wait_recv()
            if k != 3:
                @pl.when(l > 0)
                def _():
                    z_copy(t, o, 0).start()

            g_copy(t, o).start()

    def wx_copy(d, p):
        q = (y + 2 * p) % 4
        to = (x + d) % 4
        return rcopy(
            cb.at[pl.ds(2 * q, 2), to],
            W.at[pl.ds(2 * q, 2), :, :, pl.ds(128 * (4 - d), 128)],
            wx_send.at[d - 1, p], wx_recv.at[d - 1, p], wide(l, to, c),
        )

    def wx_wait(d, p):
        q = (y + 2 * p) % 4
        part = W.at[pl.ds(2 * q, 2), :, :, pl.ds(128 * (4 - d), 128)]
        rcopy(part, part, wx_send.at[d - 1, p], wx_recv.at[d - 1, p], sib).wait_recv()

    def wy_copy(d, up):
        part = W.at[pl.ds(2 * y, 2), :, :, pl.ds(128 * (4 - d), 128)]
        return rcopy(
            part, part, wy_send.at[d - 1, up], wy_recv.at[d - 1, up],
            narrow(h, (y + 2 * up + 3) % 4),
        )

    def wy_wait(d, up):
        q = (y + 5 - 2 * up) % 4
        part = W.at[pl.ds(2 * q, 2), :, :, pl.ds(128 * (4 - d), 128)]
        rcopy(part, part, wy_send.at[d - 1, up], wy_recv.at[d - 1, up], sib).wait_recv()

    def w_step(d):
        wx_wait(d, 0)
        wy_copy(d, 1).start()
        wy_copy(d, 0).start()

    for t in range(2):
        @pl.when(l < 7)
        def _():
            z_copy(t, l, 1).start()

        @pl.when(l > 0)
        def _():
            z_copy(t, l, 0).start()

        @pl.when(l < 4)
        def _():
            z_jump(t, 1).start()

        @pl.when(l >= 4)
        def _():
            z_jump(t, 0).start()

        if t == 0:
            for d in (1, 3, 2):
                wx_copy(d, 0).start()
        g_copy(t, l).start()
    for d in (1, 3, 2):
        wx_copy(d, 1).start()

    for i in range(3, 7):
        loads[i].wait()

    @pl.loop(0, 8)
    def _(i):
        CT[i] = cycV[i].T

    spec[...] = jnp.broadcast_to(cycrV[...], (128, 256)).T * cellV[...] + noiseV[...]

    for t, k in ((0, 1), (0, 4), (1, 1), (0, 2), (1, 4)):
        z_step(t, k)
    w_step(1)
    w_step(3)
    for t, k in ((0, 5), (1, 2), (0, 3)):
        z_step(t, k)
    w_step(2)
    for t, k in ((1, 5), (0, 6), (1, 3), (0, 7), (1, 6)):
        z_step(t, k)

    loads[2].wait()
    for d in (1, 3, 2):
        wx_wait(d, 1)
        wy_wait(d, 0)
        wy_wait(d, 1)

    def mac(t, o):
        g_wait(t, o)
        block = jnp.concatenate([G[t, o, 0], G[t, o, 1]], axis=1)
        acc[t] += dot_nn(block, W[o].reshape(256, 512))

    def xr_copy(t, d):
        return rcopy(
            XS.at[t, d - 1], XR.at[t, d - 1], xr_send.at[t, d - 1], xr_recv.at[t, d - 1],
            wide(l, (x + d) % 4, c),
        )

    def send_partials(t):
        for d in (2, 1, 3):
            XS[t, d - 1] = acc[t, :, 128 * d : 128 * d + 128].astype(BF16)
            xr_copy(t, d).start()

    acc[...] = jnp.zeros_like(acc)

    @pl.loop(0, 8)
    def _(o):
        mac(0, o)

    send_partials(0)

    z_step(1, 7)
    mac(1, l)

    @pl.loop(1, 8)
    def _(k):
        mac(1, (l + k) % 8)

    send_partials(1)

    def h_copy(t):
        return rcopy(PF.at[t, n], PF.at[t, n], h_sem.at[t, 0], h_sem.at[t, 1], h_peer)

    def h_wait(t):
        rcopy(
            PF.at[t, n_peer], PF.at[t, n_peer], h_sem.at[t, 0], h_sem.at[t, 1], h_peer
        ).wait_recv()

    def y_copy(t, rel, d):
        m = ((h + rel) % 2) * 4 + y
        return rcopy(
            PF.at[t, m], PF.at[t, m], y_send.at[t, rel, d - 1], y_recv.at[t, rel, d - 1],
            narrow(h, (y + d) % 4),
        )

    def y_wait(t, rel, d):
        m = ((h + rel) % 2) * 4 + (y + 4 - d) % 4
        rcopy(
            PF.at[t, m], PF.at[t, m], y_send.at[t, rel, d - 1], y_recv.at[t, rel, d - 1],
            narrow(h, (y + d) % 4),
        ).wait_recv()

    def finish_proj(t):
        total = acc[t, :, :128]
        for d in (1, 3, 2):
            xr_copy(t, d).wait_recv()
            total = total + XR[t, d - 1].astype(F32)
        PF[t, n] = total.astype(BF16).reshape(4, 2, 32, 128)
        h_copy(t).start()
        for d in (2, 1, 3):
            y_copy(t, 0, d).start()

    def pass_on(t):
        h_wait(t)
        for d in (2, 1, 3):
            y_copy(t, 1, d).start()

    def pb_copy(t):
        return rcopy(PF.at[t, :, :, 1 - c], PB.at[t], pb_sem.at[t, 0], pb_sem.at[t, 1], sib)

    def k_copy(t):
        return rcopy(KO.at[t], KS.at[t], k_sem.at[t, 0], k_sem.at[t, 1], sib)

    def rotate(t):
        for rel in range(2):
            for d in range(1, 4):
                y_wait(t, rel, d)
        pb_copy(t).start()
        rot = jnp.zeros((256, 128), F32)
        for m in range(8):
            rot = rot + dot_nn(CT[m], PF[t, m].reshape(256, 128))
        KO[t] = (rot / spec[...]).astype(BF16)
        k_copy(t).start()

    finish_proj(0)
    finish_proj(1)
    pass_on(0)
    rotate(0)
    coef_out[...] = KO[0]
    pass_on(1)
    rotate(1)

    for t in range(2):
        pb_copy(t).wait_recv()
        k_copy(t).wait_recv()

    def rows(xx):
        q = dot_nt(PF[1, :, xx, c].reshape(256, 128), KO[0])
        q = q + dot_nt(PF[0, :, xx, c].reshape(256, 128), KO[1])
        q = q + dot_nt(PB[1, :, xx].reshape(256, 128), KS[0])
        q = q + dot_nt(PB[0, :, xx].reshape(256, 128), KS[1])
        return q.reshape(8, 32, 256)

    def qx_copy(d):
        return rcopy(
            QS.at[d - 1], QR.at[d - 1], qx_send.at[d - 1], qx_recv.at[d - 1],
            wide(l, (x + d) % 4, c),
        )

    for d in (2, 1, 3):
        QS[d - 1] = rows((x + d) % 4).astype(BF16)
        qx_copy(d).start()
    Q[...] = rows(x)
    for d in (1, 3, 2):
        qx_copy(d).wait_recv()
    R[...] = Q[...] + QR[0].astype(F32) + QR[2].astype(F32) + QR[1].astype(F32)
    RS[...] = R[...].astype(BF16)

    def rz_copy(k):
        to = (l + k) % 8
        return rcopy(RS.at[to], RR.at[l], rz_send.at[k], rz_recv.at[l], wide(to, x, c))

    def rz_wait(k):
        frm = (l + k) % 8
        rcopy(RR.at[frm], RR.at[frm], rz_send.at[k], rz_recv.at[frm], wide(frm, x, c)).wait_recv()

    @pl.loop(1, 8)
    def _(k):
        rz_copy(k).start()

    grad_out[...] = R[l]

    @pl.loop(1, 8)
    def _(k):
        rz_wait(k)
        grad_out[...] += RR[(l + k) % 8].astype(F32)

    def drain_gather():
        for t in range(2):
            @pl.loop(0, 8)
            def _(o):
                @pl.when(jnp.logical_and(jnp.logical_and(o <= l, l < 7), l - o != 3))
                def _():
                    z_copy(t, o, 1).wait_send()

                @pl.when(jnp.logical_and(jnp.logical_and(o >= l, l > 0), o - l != 3))
                def _():
                    z_copy(t, o, 0).wait_send()

                g_copy(t, o).wait_send()

            @pl.when(l < 4)
            def _():
                z_jump(t, 1).wait_send()

            @pl.when(l >= 4)
            def _():
                z_jump(t, 0).wait_send()

            for d in range(1, 4):
                wx_copy(d, t).wait_send()
                wy_copy(d, t).wait_send()

    def drain_partials():
        for t in range(2):
            for d in range(1, 4):
                xr_copy(t, d).wait_send()

    def drain_proj():
        for t in range(2):
            h_copy(t).wait_send()
            for rel in range(2):
                for d in range(1, 4):
                    y_copy(t, rel, d).wait_send()
            pb_copy(t).wait_send()
            k_copy(t).wait_send()

    drain_gather()
    drain_partials()
    drain_proj()
    for d in range(1, 4):
        qx_copy(d).wait_send()

    @pl.loop(1, 8)
    def _(k):
        rz_copy(k).wait_send()


def on_device(obs, cot, cell_basis, cycle_basis, cell_spectrum, cycle_spectrum, noise_var):
    vmem = pl.BlockSpec(memory_space=pltpu.VMEM)
    dma = pltpu.SemaphoreType.DMA
    return pl.pallas_call(
        kernel,
        out_shape=(
            jax.ShapeDtypeStruct((256, 128), BF16),
            jax.ShapeDtypeStruct((32, 256), F32),
        ),
        in_specs=[pl.BlockSpec(memory_space=pltpu.HBM)] * 7,
        out_specs=(vmem, vmem),
        scratch_shapes=[
            pltpu.VMEM((2, 8, 2, 256, 128), BF16),
            pltpu.VMEM((8, 2, 128, 512), BF16),
            pltpu.VMEM((2, 256, 512), F32),
            pltpu.VMEM((2, 3, 256, 128), BF16),
            pltpu.VMEM((2, 3, 256, 128), BF16),
            pltpu.VMEM((2, 8, 4, 2, 32, 128), BF16),
            pltpu.VMEM((2, 8, 4, 32, 128), BF16),
            pltpu.VMEM((8, 256, 256), BF16),
            pltpu.VMEM((8, 256, 256), BF16),
            pltpu.VMEM((1, 128), F32),
            pltpu.VMEM((1, 256), F32),
            pltpu.VMEM((1, 1), F32),
            pltpu.VMEM((256, 128), F32),
            pltpu.VMEM((2, 256, 128), BF16),
            pltpu.VMEM((2, 256, 128), BF16),
            pltpu.VMEM((8, 32, 256), F32),
            pltpu.VMEM((3, 8, 32, 256), BF16),
            pltpu.VMEM((3, 8, 32, 256), BF16),
            pltpu.VMEM((8, 32, 256), F32),
            pltpu.VMEM((8, 32, 256), BF16),
            pltpu.VMEM((8, 32, 256), BF16),
            dma((7,)),
            dma((2, 8, 2)), dma((2, 2)), dma((2, 8)),
            dma((2, 8)), dma((2, 8)),
            dma((3, 2)), dma((3, 2)),
            dma((3, 2)), dma((3, 2)),
            dma((2, 3)), dma((2, 3)),
            dma((2, 2)),
            dma((2, 2, 3)), dma((2, 2, 3)),
            dma((2, 2)), dma((2, 2)),
            dma((3,)), dma((3,)),
            dma((8,)), dma((8,)),
        ],
        compiler_params=pltpu.CompilerParams(
            collective_id=0, has_side_effects=True, vmem_limit_bytes=60 << 20
        ),
    )(
        obs,
        cot,
        cell_basis.reshape(8, 4, 2, 128, 128),
        cycle_basis.reshape(8, 256, 256),
        cell_spectrum.reshape(1, 128),
        cycle_spectrum.reshape(1, 256),
        noise_var.reshape(1, 1),
    )


def solution(mesh):
    in_specs = (
        P("narrow", "wide"),
        P("narrow", "wide"),
        P(None, "wide"),
        P(None, "narrow"),
        P("wide"),
        P("narrow"),
        P(),
    )
    out_specs = (P("narrow", "wide"), P("wide", "narrow"))
    return jax.shard_map(
        on_device, mesh=mesh, in_specs=in_specs, out_specs=out_specs, check_vma=False
    )
```

```python
import jax
import jax.numpy as jnp
from jax import lax
from jax.experimental import pallas as pl
from jax.experimental.pallas import tpu as pltpu
from jax.sharding import PartitionSpec as P

F32 = jnp.float32
BF16 = jnp.bfloat16
MESH = pl.DeviceIdType.MESH


def dot_nt(left, right):
    return lax.dot_general(left, right, (((1,), (1,)), ((), ())), preferred_element_type=F32)


def dot_nn(left, right):
    return lax.dot_general(left, right, (((1,), (0,)), ((), ())), preferred_element_type=F32)


def kernel(
    obs, cot, cb, cyc, cell_row, cyc_row, noise,
    coef_out, grad_out,
    G, W, acc, XS, XR, PF, PB, cycV, CT, cellV, cycrV, noiseS, spec, KO, KS,
    Q, QS, QR, R, RS, RR,
    in_sem, g0_sem, z_send, z_recv, g_send, g_recv,
    wx_send, wx_recv, wy_send, wy_recv, xr_send, xr_recv,
    y_send, y_recv, pb_sem, k_sem, qx_send, qx_recv, rz_send, rz_recv,
):
    w = lax.axis_index("wide")
    n = lax.axis_index("narrow")
    l, x, c = w // 8, (w // 2) % 4, w % 2
    h, y = n // 4, n % 4
    z = h * 8 + l
    s = 1 - 2 * c

    def wide(l_, x_, c_):
        return {"wide": (l_ * 4 + x_) * 2 + c_}

    def narrow(h_, y_):
        return {"narrow": h_ * 4 + y_}

    def along_z(z_):
        return {"wide": ((z_ % 8) * 4 + x) * 2 + c, "narrow": (z_ // 8) * 4 + y}

    sib = wide(l, x, 1 - c)

    def rcopy(src, dst, ss, rs, dev):
        return pltpu.make_async_remote_copy(
            src_ref=src, dst_ref=dst, send_sem=ss, recv_sem=rs, device_id=dev, device_id_type=MESH
        )

    bar = pltpu.get_barrier_semaphore()

    def greet(dev):
        pl.semaphore_signal(bar, inc=1, device_id=dev, device_id_type=MESH)

    for d in (2, 1, 3):
        greet(wide(l, (x + d) % 4, c))
        greet(narrow(h, (y + d) % 4))
    greet(along_z((z - 2 * s + 16) % 16))
    greet(along_z((z - s + 16) % 16))
    greet(sib)

    loads = [
        pltpu.make_async_copy(obs, G.at[0, z, c], in_sem.at[0]),
        pltpu.make_async_copy(cot, G.at[1, z, c], in_sem.at[1]),
        pltpu.make_async_copy(cb.at[:, x], W.at[:, :, :, pl.ds(0, 128)], in_sem.at[2]),
        pltpu.make_async_copy(cyc, cycV, in_sem.at[3]),
        pltpu.make_async_copy(cell_row, cellV, in_sem.at[4]),
        pltpu.make_async_copy(cyc_row, cycrV, in_sem.at[5]),
        pltpu.make_async_copy(noise, noiseS, in_sem.at[6]),
    ]
    for load in loads:
        load.start()
    loads[0].wait()
    loads[1].wait()
    pl.semaphore_wait(bar, 9)

    def z_copy(t, o, q, hop=1):
        part = G.at[t, o, q]
        return rcopy(
            part, part, z_send.at[t, o, q, hop - 1], z_recv.at[t, o, q],
            along_z((z + hop * s + 16) % 16),
        )

    def g0_copy(t):
        return rcopy(G.at[t, z, c], G.at[t, z, c], g0_sem.at[t, 0], g0_sem.at[t, 1], sib)

    def g0_wait(t):
        part = G.at[t, z, 1 - c]
        rcopy(part, part, g0_sem.at[t, 0], g0_sem.at[t, 1], sib).wait_recv()

    def g_copy(t, o):
        return rcopy(G.at[t, o], G.at[t, o], g_send.at[t, o], g_recv.at[t, o], sib)

    def origin(k):
        return (z - s * k + 16) % 16

    def hops(k):
        return {1: (2, 1), 2: ()}.get(k, (1,) if k < 8 else ())

    def z_step(t, k):
        def go():
            o = origin(k)
            for q in (c, 1 - c):
                z_copy(t, o, q).wait_recv()

                def send():
                    for hop in hops(k):
                        z_copy(t, o, q, hop).start()

                if k == 7:
                    pl.when(c == t)(send)
                else:
                    send()

            g_copy(t, o).start()

        if k < 8:
            go()
        else:
            pl.when(c == t)(go)

    def wx_copy(d, p):
        q = (y + 2 * p) % 4
        to = (x + d) % 4
        return rcopy(
            cb.at[pl.ds(2 * q, 2), to],
            W.at[pl.ds(2 * q, 2), :, :, pl.ds(128 * (4 - d), 128)],
            wx_send.at[d - 1, p], wx_recv.at[d - 1, p], wide(l, to, c),
        )

    def wx_wait(d, p):
        q = (y + 2 * p) % 4
        part = W.at[pl.ds(2 * q, 2), :, :, pl.ds(128 * (4 - d), 128)]
        rcopy(part, part, wx_send.at[d - 1, p], wx_recv.at[d - 1, p], sib).wait_recv()

    def wy_copy(d, up):
        part = W.at[pl.ds(2 * y, 2), :, :, pl.ds(128 * (4 - d), 128)]
        return rcopy(
            part, part, wy_send.at[d - 1, up], wy_recv.at[d - 1, up],
            narrow(h, (y + 2 * up + 3) % 4),
        )

    def wy_wait(d, up):
        q = (y + 5 - 2 * up) % 4
        part = W.at[pl.ds(2 * q, 2), :, :, pl.ds(128 * (4 - d), 128)]
        rcopy(part, part, wy_send.at[d - 1, up], wy_recv.at[d - 1, up], sib).wait_recv()

    def w_step(d):
        wx_wait(d, 0)
        wy_copy(d, 1).start()
        wy_copy(d, 0).start()

    for t in range(2):
        z_copy(t, z, c).start()
        g0_copy(t).start()
    for t in range(2):
        g0_wait(t)
        z_copy(t, z, 1 - c).start()
    for p in range(2):
        for d in (1, 3, 2):
            wx_copy(d, p).start()

    acc[...] = jnp.zeros_like(acc)
    for i in range(3, 7):
        loads[i].wait()

    def transpose(i):
        CT[i] = cycV[i].T

    def mac(t, o):
        block = jnp.concatenate([G[t, o, 0], G[t, o, 1]], axis=1)
        acc[t, o // 8] += dot_nn(block, W[o % 8].reshape(256, 512))

    def macs(t, k):
        if k == 0:
            mac(t, z)
        elif k < 8:
            mac(t, origin(k))
            other = (z + s * k + 16) % 16
            g_copy(t, other).wait_recv()
            mac(t, other)
        else:
            far = (z + 8) % 16

            @pl.when(c != t)
            def _():
                g_copy(t, far).wait_recv()

            mac(t, far)

    def xr_copy(t, hh, d):
        return rcopy(
            XS.at[t, d - 1, hh], XR.at[t, d - 1, hh],
            xr_send.at[t, hh, d - 1], xr_recv.at[t, hh, d - 1], wide(l, (x + d) % 4, c),
        )

    def send_partials(t):
        for hh in range(2):
            for d in (2, 1, 3):
                XS[t, d - 1, hh] = acc[t, hh, :, 128 * d : 128 * d + 128].astype(BF16)
                xr_copy(t, hh, d).start()

    def z_steps(k):
        z_step(0, k)
        z_step(1, k)

    z_steps(1)
    w_step(1)
    w_step(3)
    z_steps(2)
    w_step(2)
    for i in range(4):
        transpose(i)
    z_steps(3)
    for i in range(4, 8):
        transpose(i)
    spec[...] = jnp.broadcast_to(cycrV[...], (128, 256)).T * cellV[...] + noiseS[0]
    z_steps(4)
    loads[2].wait()
    for d in (1, 3, 2):
        wx_wait(d, 1)
        wy_wait(d, 0)
        wy_wait(d, 1)
    macs(0, 0)
    macs(1, 0)
    for k in (5, 6, 7):
        z_steps(k)
        for j in ((1, 2), (3, 4), (5, 6))[k - 5]:
            macs(0, j)
            macs(1, j)
    macs(0, 7)
    z_step(0, 8)
    macs(0, 8)
    send_partials(0)
    macs(1, 7)
    z_step(1, 8)
    macs(1, 8)
    send_partials(1)

    def y_copy(t, hh, d):
        rows_of = PF.at[t, hh, y]
        return rcopy(
            rows_of, rows_of, y_send.at[t, hh, d - 1], y_recv.at[t, hh, d - 1],
            narrow(h, (y + d) % 4),
        )

    def y_wait(t, hh, d):
        rows_of = PF.at[t, hh, (y + 4 - d) % 4]
        rcopy(rows_of, rows_of, y_send.at[t, hh, d - 1], y_recv.at[t, hh, d - 1], sib).wait_recv()

    def finish_proj(t, hh):
        total = acc[t, hh, :, :128]
        for d in (1, 3, 2):
            xr_copy(t, hh, d).wait_recv()
            total = total + XR[t, d - 1, hh].astype(F32)
        PF[t, hh, y] = total.astype(BF16).reshape(4, 2, 32, 128)
        for d in (2, 1, 3):
            y_copy(t, hh, d).start()

    def pb_copy(t):
        return rcopy(PF.at[t, :, :, :, 1 - c], PB.at[t], pb_sem.at[t, 0], pb_sem.at[t, 1], sib)

    def k_copy(t):
        return rcopy(KO.at[t], KS.at[t], k_sem.at[t, 0], k_sem.at[t, 1], sib)

    def rotate(t):
        for hh in range(2):
            for d in (1, 3, 2):
                y_wait(t, hh, d)
        pb_copy(t).start()
        rot = jnp.zeros((256, 128), F32)
        for m in range(8):
            rot = rot + dot_nn(CT[m], PF[t, m // 4, m % 4].reshape(256, 128))
        KO[t] = (rot / spec[...]).astype(BF16)
        k_copy(t).start()

    for t in range(2):
        for hh in range(2):
            finish_proj(t, hh)
    rotate(0)
    coef_out[...] = KO[0]
    rotate(1)

    for t in range(2):
        pb_copy(t).wait_recv()
        k_copy(t).wait_recv()

    def rows(xx, g):
        q = dot_nt(PF[1, g, :, xx, c].reshape(128, 128), KO[0])
        q = q + dot_nt(PF[0, g, :, xx, c].reshape(128, 128), KO[1])
        q = q + dot_nt(PB[1, g, :, xx].reshape(128, 128), KS[0])
        q = q + dot_nt(PB[0, g, :, xx].reshape(128, 128), KS[1])
        return q.reshape(4, 32, 256)

    def qx_copy(g, d):
        return rcopy(
            QS.at[d - 1, g], QR.at[d - 1, g], qx_send.at[g, d - 1], qx_recv.at[g, d - 1],
            wide(l, (x + d) % 4, c),
        )

    def rz_copy(to):
        return rcopy(RS.at[to], RR.at[l], rz_send.at[to], rz_recv.at[l], wide(to, x, c))

    def rz_wait(frm):
        rcopy(
            RR.at[frm], RR.at[frm], rz_send.at[frm], rz_recv.at[frm], wide(frm, x, c)
        ).wait_recv()

    for g in range(2):
        for d in (2, 1, 3):
            QS[d - 1, g] = rows((x + d) % 4, g).astype(BF16)
            qx_copy(g, d).start()
        Q[g] = rows(x, g)
    for g in range(2):
        for d in (1, 3, 2):
            qx_copy(g, d).wait_recv()
        total = Q[g] + QR[0, g].astype(F32) + QR[2, g].astype(F32) + QR[1, g].astype(F32)
        R[4 * g : 4 * g + 4] = total
        RS[4 * g : 4 * g + 4] = total.astype(BF16)
        for to in range(4 * g, 4 * g + 4):
            @pl.when(l != to)
            def _():
                rz_copy(to).start()

    grad_out[...] = R[l]

    @pl.loop(1, 8)
    def _(k):
        rz_wait((l + k) % 8)
        grad_out[...] += RR[(l + k) % 8].astype(F32)

    def drain_gather():
        for t in range(2):
            g0_copy(t).wait_send()
            for q in range(2):
                z_copy(t, z, q).wait_send()

            for k in range(1, 8):
                o = origin(k)
                g_copy(t, o).wait_send()
                for hop in hops(k):
                    def left():
                        for q in range(2):
                            z_copy(t, o, q, hop).wait_send()

                    if k == 7:
                        pl.when(c == t)(left)
                    else:
                        left()

            @pl.when(c == t)
            def _():
                g_copy(t, (z + 8) % 16).wait_send()

            for d in range(1, 4):
                wx_copy(d, t).wait_send()
                wy_copy(d, t).wait_send()

    def drain_partials():
        for t in range(2):
            for hh in range(2):
                for d in range(1, 4):
                    xr_copy(t, hh, d).wait_send()

    def drain_proj():
        for t in range(2):
            for hh in range(2):
                for d in range(1, 4):
                    y_copy(t, hh, d).wait_send()
            pb_copy(t).wait_send()
            k_copy(t).wait_send()

    drain_gather()
    drain_partials()
    drain_proj()
    for g in range(2):
        for d in range(1, 4):
            qx_copy(g, d).wait_send()

    @pl.loop(1, 8)
    def _(k):
        rz_copy((l + k) % 8).wait_send()


def on_device(obs, cot, cell_basis, cycle_basis, cell_spectrum, cycle_spectrum, noise_var):
    vmem = pl.BlockSpec(memory_space=pltpu.VMEM)
    dma = pltpu.SemaphoreType.DMA
    return pl.pallas_call(
        kernel,
        out_shape=(
            jax.ShapeDtypeStruct((256, 128), BF16),
            jax.ShapeDtypeStruct((32, 256), F32),
        ),
        in_specs=[pl.BlockSpec(memory_space=pltpu.HBM)] * 7,
        out_specs=(vmem, vmem),
        scratch_shapes=[
            pltpu.VMEM((2, 16, 2, 256, 128), BF16),
            pltpu.VMEM((8, 2, 128, 512), BF16),
            pltpu.VMEM((2, 2, 256, 512), F32),
            pltpu.VMEM((2, 3, 2, 256, 128), BF16),
            pltpu.VMEM((2, 3, 2, 256, 128), BF16),
            pltpu.VMEM((2, 2, 4, 4, 2, 32, 128), BF16),
            pltpu.VMEM((2, 2, 4, 4, 32, 128), BF16),
            pltpu.VMEM((8, 256, 256), BF16),
            pltpu.VMEM((8, 256, 256), BF16),
            pltpu.VMEM((1, 128), F32),
            pltpu.VMEM((1, 256), F32),
            pltpu.SMEM((1,), F32),
            pltpu.VMEM((256, 128), F32),
            pltpu.VMEM((2, 256, 128), BF16),
            pltpu.VMEM((2, 256, 128), BF16),
            pltpu.VMEM((2, 4, 32, 256), F32),
            pltpu.VMEM((3, 2, 4, 32, 256), BF16),
            pltpu.VMEM((3, 2, 4, 32, 256), BF16),
            pltpu.VMEM((8, 32, 256), F32),
            pltpu.VMEM((8, 32, 256), BF16),
            pltpu.VMEM((8, 32, 256), BF16),
            dma((7,)),
            dma((2, 2)),
            dma((2, 16, 2, 2)), dma((2, 16, 2)),
            dma((2, 16)), dma((2, 16)),
            dma((3, 2)), dma((3, 2)),
            dma((3, 2)), dma((3, 2)),
            dma((2, 2, 3)), dma((2, 2, 3)),
            dma((2, 2, 3)), dma((2, 2, 3)),
            dma((2, 2)), dma((2, 2)),
            dma((2, 3)), dma((2, 3)),
            dma((8,)), dma((8,)),
        ],
        compiler_params=pltpu.CompilerParams(
            collective_id=0, has_side_effects=True, vmem_limit_bytes=60 << 20
        ),
    )(
        obs,
        cot,
        cell_basis.reshape(8, 4, 2, 128, 128),
        cycle_basis.reshape(8, 256, 256),
        cell_spectrum.reshape(1, 128),
        cycle_spectrum.reshape(1, 256),
        noise_var,
    )


def solution(mesh):
    in_specs = (
        P("narrow", "wide"),
        P("narrow", "wide"),
        P(None, "wide"),
        P(None, "narrow"),
        P("wide"),
        P("narrow"),
        P(),
    )
    out_specs = (P("narrow", "wide"), P("wide", "narrow"))
    return jax.shard_map(
        on_device, mesh=mesh, in_specs=in_specs, out_specs=out_specs, check_vma=False
    )
```

```python
import jax
import jax.numpy as jnp
from jax import lax
from jax.experimental import pallas as pl
from jax.experimental.pallas import tpu as pltpu
from jax.sharding import PartitionSpec as P

F32 = jnp.float32
BF16 = jnp.bfloat16
MESH = pl.DeviceIdType.MESH


def dot_nt(left, right):
    return lax.dot_general(left, right, (((1,), (1,)), ((), ())), preferred_element_type=F32)


def dot_nn(left, right):
    return lax.dot_general(left, right, (((1,), (0,)), ((), ())), preferred_element_type=F32)


def kernel(
    obs, cot, cb, cyc, cell_row, cyc_row, noise,
    coef_out, grad_out,
    G, W, acc, XS, XR, PF, PB, cycV, CT, cellV, cycrV, noiseS, spec, KO, KS,
    Q, QS, QR, R, RS, RR,
    in_sem, g0_sem, z_send, z_recv, g_send, g_recv,
    wx_send, wx_recv, wy_send, wy_recv, xr_send, xr_recv,
    y_send, y_recv, pb_sem, k_sem, qx_send, qx_recv, rz_send, rz_recv,
):
    w = lax.axis_index("wide")
    n = lax.axis_index("narrow")
    l, x, c = w // 8, (w // 2) % 4, w % 2
    h, y = n // 4, n % 4
    z = h * 8 + l
    s = 1 - 2 * c

    def wide(l_, x_, c_):
        return {"wide": (l_ * 4 + x_) * 2 + c_}

    def narrow(h_, y_):
        return {"narrow": h_ * 4 + y_}

    def along_z(z_):
        return {"wide": ((z_ % 8) * 4 + x) * 2 + c, "narrow": (z_ // 8) * 4 + y}

    sib = wide(l, x, 1 - c)

    def rcopy(src, dst, ss, rs, dev):
        return pltpu.make_async_remote_copy(
            src_ref=src, dst_ref=dst, send_sem=ss, recv_sem=rs, device_id=dev, device_id_type=MESH
        )

    bar = pltpu.get_barrier_semaphore()

    def greet(dev):
        pl.semaphore_signal(bar, inc=1, device_id=dev, device_id_type=MESH)

    for d in (2, 1, 3):
        greet(wide(l, (x + d) % 4, c))
        greet(narrow(h, (y + d) % 4))
    greet(along_z((z - s + 16) % 16))
    greet(sib)

    loads = [
        pltpu.make_async_copy(obs, G.at[z, 0, c], in_sem.at[0]),
        pltpu.make_async_copy(cot, G.at[z, 1, c], in_sem.at[1]),
        pltpu.make_async_copy(cb.at[:, x], W.at[:, :, :, pl.ds(0, 128)], in_sem.at[2]),
        pltpu.make_async_copy(cyc, cycV, in_sem.at[3]),
        pltpu.make_async_copy(cell_row, cellV, in_sem.at[4]),
        pltpu.make_async_copy(cyc_row, cycrV, in_sem.at[5]),
        pltpu.make_async_copy(noise, noiseS, in_sem.at[6]),
    ]
    for load in loads:
        load.start()
    loads[0].wait()
    loads[1].wait()
    pl.semaphore_wait(bar, 8)

    def z_copy(t, o, q):
        part = G.at[o, t, q]
        return rcopy(
            part, part, z_send.at[t, o, q], z_recv.at[t, o, q], along_z((z + s + 16) % 16)
        )

    def g0_copy(t):
        return rcopy(G.at[z, t, c], G.at[z, t, c], g0_sem.at[t, 0], g0_sem.at[t, 1], sib)

    def g0_wait(t):
        part = G.at[z, t, 1 - c]
        rcopy(part, part, g0_sem.at[t, 0], g0_sem.at[t, 1], sib).wait_recv()

    def g_copy(o):
        return rcopy(G.at[o], G.at[o], g_send.at[o], g_recv.at[o], sib)

    def g_far(t):
        far = (z + 8) % 16
        return rcopy(G.at[far, t], G.at[far, t], g_send.at[far], g_recv.at[far], sib)

    def origin(k):
        return (z - s * k + 16) % 16

    def z_step(t, k):
        def go():
            o = origin(k)
            for q in (c, 1 - c):
                z_copy(t, o, q).wait_recv()

                def send():
                    z_copy(t, o, q).start()

                if k < 7:
                    send()
                elif k == 7:
                    pl.when(c == t)(send)

            if k == 8:
                g_far(t).start()

        if k < 8:
            go()
        else:
            pl.when(c == t)(go)

    def wx_copy(d, p):
        q = (y + 2 * p) % 4
        to = (x + d) % 4
        return rcopy(
            cb.at[pl.ds(2 * q, 2), to],
            W.at[pl.ds(2 * q, 2), :, :, pl.ds(128 * (4 - d), 128)],
            wx_send.at[d - 1, p], wx_recv.at[d - 1, p], wide(l, to, c),
        )

    def wx_wait(d, p):
        q = (y + 2 * p) % 4
        part = W.at[pl.ds(2 * q, 2), :, :, pl.ds(128 * (4 - d), 128)]
        rcopy(part, part, wx_send.at[d - 1, p], wx_recv.at[d - 1, p], sib).wait_recv()

    def wy_copy(d, up):
        part = W.at[pl.ds(2 * y, 2), :, :, pl.ds(128 * (4 - d), 128)]
        return rcopy(
            part, part, wy_send.at[d - 1, up], wy_recv.at[d - 1, up],
            narrow(h, (y + 2 * up + 3) % 4),
        )

    def wy_wait(d, up):
        q = (y + 5 - 2 * up) % 4
        part = W.at[pl.ds(2 * q, 2), :, :, pl.ds(128 * (4 - d), 128)]
        rcopy(part, part, wy_send.at[d - 1, up], wy_recv.at[d - 1, up], sib).wait_recv()

    def w_step(d):
        wx_wait(d, 0)
        wy_copy(d, 1).start()
        wy_copy(d, 0).start()

    for t in range(2):
        z_copy(t, z, c).start()
        g0_copy(t).start()
    for t in range(2):
        g0_wait(t)
        z_copy(t, z, 1 - c).start()
    for p in range(2):
        for d in (1, 3, 2):
            wx_copy(d, p).start()

    acc[...] = jnp.zeros_like(acc)
    for i in range(3, 7):
        loads[i].wait()

    def transpose(i):
        CT[i] = cycV[i].T

    def mac(t, o):
        block = jnp.concatenate([G[o, t, 0], G[o, t, 1]], axis=1)
        acc[t, o // 8] += dot_nn(block, W[o % 8].reshape(256, 512))

    def macs(t, k):
        if k == 0:
            mac(t, z)
        elif k < 8:
            mac(t, origin(k))
            other = (z + s * k + 16) % 16
            if t == 0:
                g_copy(other).wait_recv()
            mac(t, other)
        else:
            far = (z + 8) % 16

            @pl.when(c != t)
            def _():
                g_far(t).wait_recv()

            mac(t, far)

    def xr_copy(t, hh, d):
        return rcopy(
            XS.at[t, d - 1, hh], XR.at[t, d - 1, hh],
            xr_send.at[t, hh, d - 1], xr_recv.at[t, hh, d - 1], wide(l, (x + d) % 4, c),
        )

    def send_partials(t):
        for hh in range(2):
            for d in (2, 1, 3):
                XS[t, d - 1, hh] = acc[t, hh, :, 128 * d : 128 * d + 128].astype(BF16)
                xr_copy(t, hh, d).start()

    def z_steps(k):
        z_step(0, k)
        z_step(1, k)
        g_copy(origin(k)).start()

    z_steps(1)
    w_step(1)
    w_step(3)
    z_steps(2)
    w_step(2)
    for i in range(4):
        transpose(i)
    z_steps(3)
    for i in range(4, 8):
        transpose(i)
    spec[...] = jnp.broadcast_to(cycrV[...], (128, 256)).T * cellV[...] + noiseS[0]
    z_steps(4)
    loads[2].wait()
    for d in (1, 3, 2):
        wx_wait(d, 1)
        wy_wait(d, 0)
        wy_wait(d, 1)
    macs(0, 0)
    macs(1, 0)
    for k in (5, 6, 7):
        z_steps(k)
        for j in ((1, 2), (3, 4), (5, 6))[k - 5]:
            macs(0, j)
            macs(1, j)
    macs(0, 7)
    z_step(0, 8)
    macs(0, 8)
    send_partials(0)
    macs(1, 7)
    z_step(1, 8)
    macs(1, 8)
    send_partials(1)

    def y_copy(t, hh, d):
        rows_of = PF.at[t, hh, y]
        return rcopy(
            rows_of, rows_of, y_send.at[t, hh, d - 1], y_recv.at[t, hh, d - 1],
            narrow(h, (y + d) % 4),
        )

    def y_wait(t, hh, d):
        rows_of = PF.at[t, hh, (y + 4 - d) % 4]
        rcopy(rows_of, rows_of, y_send.at[t, hh, d - 1], y_recv.at[t, hh, d - 1], sib).wait_recv()

    def finish_proj(t, hh):
        total = acc[t, hh, :, :128]
        for d in (1, 3, 2):
            xr_copy(t, hh, d).wait_recv()
            total = total + XR[t, d - 1, hh].astype(F32)
        PF[t, hh, y] = total.astype(BF16).reshape(4, 2, 32, 128)
        for d in (2, 1, 3):
            y_copy(t, hh, d).start()

    def pb_copy(t):
        return rcopy(PF.at[t, :, :, :, 1 - c], PB.at[t], pb_sem.at[t, 0], pb_sem.at[t, 1], sib)

    def k_copy(t):
        return rcopy(KO.at[t], KS.at[t], k_sem.at[t, 0], k_sem.at[t, 1], sib)

    def rotate(t):
        for hh in range(2):
            for d in (1, 3, 2):
                y_wait(t, hh, d)
        pb_copy(t).start()
        rot = jnp.zeros((256, 128), F32)
        for m in range(8):
            rot = rot + dot_nn(CT[m], PF[t, m // 4, m % 4].reshape(256, 128))
        KO[t] = (rot / spec[...]).astype(BF16)
        k_copy(t).start()

    for t in range(2):
        for hh in range(2):
            finish_proj(t, hh)
    rotate(0)
    coef_out[...] = KO[0]
    rotate(1)

    for t in range(2):
        pb_copy(t).wait_recv()
        k_copy(t).wait_recv()

    def rows(xx, g):
        q = dot_nt(PF[1, g, :, xx, c].reshape(128, 128), KO[0])
        q = q + dot_nt(PF[0, g, :, xx, c].reshape(128, 128), KO[1])
        q = q + dot_nt(PB[1, g, :, xx].reshape(128, 128), KS[0])
        q = q + dot_nt(PB[0, g, :, xx].reshape(128, 128), KS[1])
        return q.reshape(4, 32, 256)

    def qx_copy(g, d):
        return rcopy(
            QS.at[d - 1, g], QR.at[d - 1, g], qx_send.at[g, d - 1], qx_recv.at[g, d - 1],
            wide(l, (x + d) % 4, c),
        )

    def rz_copy(to):
        return rcopy(RS.at[to], RR.at[l], rz_send.at[to], rz_recv.at[l], wide(to, x, c))

    def rz_wait(frm):
        rcopy(
            RR.at[frm], RR.at[frm], rz_send.at[frm], rz_recv.at[frm], wide(frm, x, c)
        ).wait_recv()

    for g in range(2):
        for d in (2, 1, 3):
            QS[d - 1, g] = rows((x + d) % 4, g).astype(BF16)
            qx_copy(g, d).start()
        Q[g] = rows(x, g)
    for g in range(2):
        for d in (1, 3, 2):
            qx_copy(g, d).wait_recv()
        total = Q[g] + QR[0, g].astype(F32) + QR[2, g].astype(F32) + QR[1, g].astype(F32)
        R[4 * g : 4 * g + 4] = total
        RS[4 * g : 4 * g + 4] = total.astype(BF16)
        for to in range(4 * g, 4 * g + 4):
            @pl.when(l != to)
            def _():
                rz_copy(to).start()

    grad_out[...] = R[l]

    @pl.loop(1, 8)
    def _(k):
        rz_wait((l + k) % 8)
        grad_out[...] += RR[(l + k) % 8].astype(F32)

    def drain_gather():
        for t in range(2):
            g0_copy(t).wait_send()
            for q in range(2):
                z_copy(t, z, q).wait_send()

            for k in range(1, 8):
                o = origin(k)
                if t == 0:
                    g_copy(o).wait_send()

                def left():
                    for q in range(2):
                        z_copy(t, o, q).wait_send()

                if k < 7:
                    left()
                else:
                    pl.when(c == t)(left)

            @pl.when(c == t)
            def _():
                g_far(t).wait_send()

            for d in range(1, 4):
                wx_copy(d, t).wait_send()
                wy_copy(d, t).wait_send()

    def drain_partials():
        for t in range(2):
            for hh in range(2):
                for d in range(1, 4):
                    xr_copy(t, hh, d).wait_send()

    def drain_proj():
        for t in range(2):
            for hh in range(2):
                for d in range(1, 4):
                    y_copy(t, hh, d).wait_send()
            pb_copy(t).wait_send()
            k_copy(t).wait_send()

    drain_gather()
    drain_partials()
    drain_proj()
    for g in range(2):
        for d in range(1, 4):
            qx_copy(g, d).wait_send()

    @pl.loop(1, 8)
    def _(k):
        rz_copy((l + k) % 8).wait_send()


def hand_over(coef_in, grad_in, coef_out, grad_out):
    coef_out[...] = coef_in[...]
    grad_out[...] = grad_in[...]


def on_device(obs, cot, cell_basis, cycle_basis, cell_spectrum, cycle_spectrum, noise_var):
    vmem = pl.BlockSpec(memory_space=pltpu.VMEM)
    dma = pltpu.SemaphoreType.DMA
    coefficients, basis_grad = pl.pallas_call(
        kernel,
        out_shape=(
            jax.ShapeDtypeStruct((256, 128), BF16),
            jax.ShapeDtypeStruct((32, 256), F32),
        ),
        in_specs=[pl.BlockSpec(memory_space=pltpu.HBM)] * 7,
        out_specs=(vmem, vmem),
        scratch_shapes=[
            pltpu.VMEM((16, 2, 2, 256, 128), BF16),
            pltpu.VMEM((8, 2, 128, 512), BF16),
            pltpu.VMEM((2, 2, 256, 512), F32),
            pltpu.VMEM((2, 3, 2, 256, 128), BF16),
            pltpu.VMEM((2, 3, 2, 256, 128), BF16),
            pltpu.VMEM((2, 2, 4, 4, 2, 32, 128), BF16),
            pltpu.VMEM((2, 2, 4, 4, 32, 128), BF16),
            pltpu.VMEM((8, 256, 256), BF16),
            pltpu.VMEM((8, 256, 256), BF16),
            pltpu.VMEM((1, 128), F32),
            pltpu.VMEM((1, 256), F32),
            pltpu.SMEM((1,), F32),
            pltpu.VMEM((256, 128), F32),
            pltpu.VMEM((2, 256, 128), BF16),
            pltpu.VMEM((2, 256, 128), BF16),
            pltpu.VMEM((2, 4, 32, 256), F32),
            pltpu.VMEM((3, 2, 4, 32, 256), BF16),
            pltpu.VMEM((3, 2, 4, 32, 256), BF16),
            pltpu.VMEM((8, 32, 256), F32),
            pltpu.VMEM((8, 32, 256), BF16),
            pltpu.VMEM((8, 32, 256), BF16),
            dma((7,)),
            dma((2, 2)),
            dma((2, 16, 2)), dma((2, 16, 2)),
            dma((16,)), dma((16,)),
            dma((3, 2)), dma((3, 2)),
            dma((3, 2)), dma((3, 2)),
            dma((2, 2, 3)), dma((2, 2, 3)),
            dma((2, 2, 3)), dma((2, 2, 3)),
            dma((2, 2)), dma((2, 2)),
            dma((2, 3)), dma((2, 3)),
            dma((8,)), dma((8,)),
        ],
        compiler_params=pltpu.CompilerParams(
            collective_id=0, has_side_effects=True, vmem_limit_bytes=60 << 20
        ),
    )(
        obs,
        cot,
        cell_basis.reshape(8, 4, 2, 128, 128),
        cycle_basis.reshape(8, 256, 256),
        cell_spectrum.reshape(1, 128),
        cycle_spectrum.reshape(1, 256),
        noise_var,
    )
    return pl.pallas_call(
        hand_over,
        out_shape=(
            jax.ShapeDtypeStruct((256, 128), BF16),
            jax.ShapeDtypeStruct((32, 256), F32),
        ),
        in_specs=[vmem] * 2,
        out_specs=(vmem, vmem),
    )(coefficients, basis_grad)


def solution(mesh):
    in_specs = (
        P("narrow", "wide"),
        P("narrow", "wide"),
        P(None, "wide"),
        P(None, "narrow"),
        P("wide"),
        P("narrow"),
        P(),
    )
    out_specs = (P("narrow", "wide"), P("wide", "narrow"))
    return jax.shard_map(
        on_device, mesh=mesh, in_specs=in_specs, out_specs=out_specs, check_vma=False
    )
```

```python
import jax
import jax.numpy as jnp
from jax import lax
from jax.experimental import pallas as pl
from jax.experimental.pallas import tpu as pltpu
from jax.sharding import PartitionSpec as P

F32 = jnp.float32
BF16 = jnp.bfloat16
MESH = pl.DeviceIdType.MESH


def dot_nt(left, right):
    return lax.dot_general(left, right, (((1,), (1,)), ((), ())), preferred_element_type=F32)


def dot_nn(left, right):
    return lax.dot_general(left, right, (((1,), (0,)), ((), ())), preferred_element_type=F32)


def kernel(
    obs, cot, cb, cyc, cell_row, cyc_row, noise,
    coef_out, grad_out,
    G, W, acc, XS, XR, PF, PB, cycV, CT, cellV, cycrV, noiseS, spec, KO, KS,
    Q, QS, QR, R, RS, RR,
    in_sem, g0_sem, z_send, z_recv, g_send, g_recv,
    wx_send, wx_recv, wy_send, wy_recv, xr_send, xr_recv,
    y_send, y_recv, pb_sem, k_sem, qx_send, qx_recv, rz_send, rz_recv,
):
    w = lax.axis_index("wide")
    n = lax.axis_index("narrow")
    l, x, c = w // 8, (w // 2) % 4, w % 2
    h, y = n // 4, n % 4
    z = h * 8 + l
    s = 1 - 2 * c

    def wide(l_, x_, c_):
        return {"wide": (l_ * 4 + x_) * 2 + c_}

    def narrow(h_, y_):
        return {"narrow": h_ * 4 + y_}

    def along_z(z_):
        return {"wide": ((z_ % 8) * 4 + x) * 2 + c, "narrow": (z_ // 8) * 4 + y}

    sib = wide(l, x, 1 - c)

    def rcopy(src, dst, ss, rs, dev):
        return pltpu.make_async_remote_copy(
            src_ref=src, dst_ref=dst, send_sem=ss, recv_sem=rs, device_id=dev, device_id_type=MESH
        )

    bar = pltpu.get_barrier_semaphore()

    def greet(dev):
        pl.semaphore_signal(bar, inc=1, device_id=dev, device_id_type=MESH)

    for d in (2, 1, 3):
        greet(wide(l, (x + d) % 4, c))
        greet(narrow(h, (y + d) % 4))
    greet(along_z((z - s + 16) % 16))
    greet(sib)

    loads = [
        pltpu.make_async_copy(obs, G.at[z, 0, c], in_sem.at[0]),
        pltpu.make_async_copy(cot, G.at[z, 1, c], in_sem.at[1]),
        pltpu.make_async_copy(cb.at[:, x], W.at[:, :, :, pl.ds(0, 128)], in_sem.at[2]),
        pltpu.make_async_copy(cyc, cycV, in_sem.at[3]),
        pltpu.make_async_copy(cell_row, cellV, in_sem.at[4]),
        pltpu.make_async_copy(cyc_row, cycrV, in_sem.at[5]),
        pltpu.make_async_copy(noise, noiseS, in_sem.at[6]),
    ]
    for load in loads:
        load.start()
    loads[0].wait()
    loads[1].wait()
    pl.semaphore_wait(bar, 8)

    def z_copy(t, o, q):
        part = G.at[o, t, q]
        return rcopy(
            part, part, z_send.at[t, o, q], z_recv.at[t, o, q], along_z((z + s + 16) % 16)
        )

    def g0_copy(t):
        return rcopy(G.at[z, t, c], G.at[z, t, c], g0_sem.at[t, 0], g0_sem.at[t, 1], sib)

    def g0_wait(t):
        part = G.at[z, t, 1 - c]
        rcopy(part, part, g0_sem.at[t, 0], g0_sem.at[t, 1], sib).wait_recv()

    def g_copy(o):
        return rcopy(G.at[o], G.at[o], g_send.at[o], g_recv.at[o], sib)

    def g_far(t):
        far = (z + 8) % 16
        return rcopy(G.at[far, t], G.at[far, t], g_send.at[far], g_recv.at[far], sib)

    def origin(k):
        return (z - s * k + 16) % 16

    def z_step(t, k):
        def go():
            o = origin(k)
            for q in (c, 1 - c):
                z_copy(t, o, q).wait_recv()

                def send():
                    z_copy(t, o, q).start()

                if k < 7:
                    send()
                elif k == 7:
                    pl.when(c == t)(send)

            if k == 8:
                g_far(t).start()

        if k < 8:
            go()
        else:
            pl.when(c == t)(go)

    def wx_copy(d, p):
        q = (y + 2 * p) % 4
        to = (x + d) % 4
        return rcopy(
            cb.at[pl.ds(2 * q, 2), to],
            W.at[pl.ds(2 * q, 2), :, :, pl.ds(128 * (4 - d), 128)],
            wx_send.at[d - 1, p], wx_recv.at[d - 1, p], wide(l, to, c),
        )

    def wx_wait(d, p):
        q = (y + 2 * p) % 4
        part = W.at[pl.ds(2 * q, 2), :, :, pl.ds(128 * (4 - d), 128)]
        rcopy(part, part, wx_send.at[d - 1, p], wx_recv.at[d - 1, p], sib).wait_recv()

    def wy_copy(d, up):
        part = W.at[pl.ds(2 * y, 2), :, :, pl.ds(128 * (4 - d), 128)]
        return rcopy(
            part, part, wy_send.at[d - 1, up], wy_recv.at[d - 1, up],
            narrow(h, (y + 2 * up + 3) % 4),
        )

    def wy_wait(d, up):
        q = (y + 5 - 2 * up) % 4
        part = W.at[pl.ds(2 * q, 2), :, :, pl.ds(128 * (4 - d), 128)]
        rcopy(part, part, wy_send.at[d - 1, up], wy_recv.at[d - 1, up], sib).wait_recv()

    def w_step(d):
        wx_wait(d, 0)
        wy_copy(d, 1).start()
        wy_copy(d, 0).start()

    for t in range(2):
        z_copy(t, z, c).start()
        g0_copy(t).start()
    for t in range(2):
        g0_wait(t)
        z_copy(t, z, 1 - c).start()
    for p in range(2):
        for d in (1, 3, 2):
            wx_copy(d, p).start()

    acc[...] = jnp.zeros_like(acc)
    for i in range(3, 7):
        loads[i].wait()

    def transpose(i):
        CT[i] = cycV[i].T

    def mac(t, o):
        block = jnp.concatenate([G[o, t, 0], G[o, t, 1]], axis=1)
        acc[o // 8, t] += dot_nn(block, W[o % 8].reshape(256, 512))

    def mac_both(o):
        block = jnp.concatenate(
            [G[o, :, 0].reshape(512, 128), G[o, :, 1].reshape(512, 128)], axis=1
        )
        part = dot_nn(block, W[o % 8].reshape(256, 512))
        acc[o // 8] += part.reshape(2, 256, 512)

    def macs(k):
        mac_both(origin(k))
        other = (z + s * k + 16) % 16
        g_copy(other).wait_recv()
        mac_both(other)

    def last_mac(t):
        z_step(t, 8)

        @pl.when(c != t)
        def _():
            g_far(t).wait_recv()

        mac(t, (z + 8) % 16)

    def xr_copy(t, hh, d):
        return rcopy(
            XS.at[t, d - 1, hh], XR.at[t, d - 1, hh],
            xr_send.at[t, hh, d - 1], xr_recv.at[t, hh, d - 1], wide(l, (x + d) % 4, c),
        )

    def send_partials(t):
        for hh in range(2):
            for d in (2, 1, 3):
                XS[t, d - 1, hh] = acc[hh, t, :, 128 * d : 128 * d + 128].astype(BF16)
                xr_copy(t, hh, d).start()

    def z_steps(k):
        z_step(0, k)
        z_step(1, k)
        g_copy(origin(k)).start()

    z_steps(1)
    w_step(1)
    w_step(3)
    z_steps(2)
    w_step(2)
    for i in range(4):
        transpose(i)
    z_steps(3)
    for i in range(4, 8):
        transpose(i)
    spec[...] = jnp.broadcast_to(cycrV[...], (128, 256)).T * cellV[...] + noiseS[0]
    z_steps(4)
    loads[2].wait()
    for d in (1, 3, 2):
        wx_wait(d, 1)
        wy_wait(d, 0)
        wy_wait(d, 1)
    mac_both(z)
    macs(1)
    for k in (5, 6, 7):
        z_steps(k)
        for j in ((2, 3), (4, 5), (6, 7))[k - 5]:
            macs(j)
    last_mac(0)
    send_partials(0)
    last_mac(1)
    send_partials(1)

    def y_copy(t, hh, d):
        rows_of = PF.at[t, hh, y]
        return rcopy(
            rows_of, rows_of, y_send.at[t, hh, d - 1], y_recv.at[t, hh, d - 1],
            narrow(h, (y + d) % 4),
        )

    def y_wait(t, hh, d):
        rows_of = PF.at[t, hh, (y + 4 - d) % 4]
        rcopy(rows_of, rows_of, y_send.at[t, hh, d - 1], y_recv.at[t, hh, d - 1], sib).wait_recv()

    def finish_proj(t, hh):
        total = acc[hh, t, :, :128]
        for d in (1, 3, 2):
            xr_copy(t, hh, d).wait_recv()
            total = total + XR[t, d - 1, hh].astype(F32)
        PF[t, hh, y] = total.astype(BF16).reshape(4, 2, 32, 128)
        for d in (2, 1, 3):
            y_copy(t, hh, d).start()

    def pb_copy(t, hh):
        return rcopy(
            PF.at[t, hh, :, :, 1 - c], PB.at[t, hh], pb_sem.at[t, hh, 0], pb_sem.at[t, hh, 1], sib
        )

    def k_copy(t):
        return rcopy(KO.at[t], KS.at[t], k_sem.at[t, 0], k_sem.at[t, 1], sib)

    def rotate(t):
        rot = jnp.zeros((256, 128), F32)
        for hh in range(2):
            for d in (1, 3, 2):
                y_wait(t, hh, d)
            pb_copy(t, hh).start()
            for yy in range(4):
                rot = rot + dot_nn(CT[4 * hh + yy], PF[t, hh, yy].reshape(256, 128))
        KO[t] = (rot / spec[...]).astype(BF16)
        k_copy(t).start()

    for t in range(2):
        for hh in range(2):
            finish_proj(t, hh)
    rotate(0)
    coef_out[...] = KO[0]
    rotate(1)

    def own_rows(xx, g):
        q = dot_nt(PF[1, g, :, xx, c].reshape(128, 128), KO[0])
        return q + dot_nt(PF[0, g, :, xx, c].reshape(128, 128), KO[1])

    def all_rows(q, xx, g):
        q = q + dot_nt(PB[1, g, :, xx].reshape(128, 128), KS[0])
        q = q + dot_nt(PB[0, g, :, xx].reshape(128, 128), KS[1])
        return q.reshape(4, 32, 256)

    def qx_copy(g, d):
        return rcopy(
            QS.at[d - 1, g], QR.at[d - 1, g], qx_send.at[g, d - 1], qx_recv.at[g, d - 1],
            wide(l, (x + d) % 4, c),
        )

    def rz_copy(to):
        return rcopy(RS.at[to], RR.at[l], rz_send.at[to], rz_recv.at[l], wide(to, x, c))

    def rz_wait(frm):
        rcopy(
            RR.at[frm], RR.at[frm], rz_send.at[frm], rz_recv.at[frm], wide(frm, x, c)
        ).wait_recv()

    for g in range(2):
        own = [own_rows((x + d) % 4, g) for d in (2, 1, 3)]
        if g == 0:
            for t in range(2):
                for hh in range(2):
                    pb_copy(t, hh).wait_recv()
                k_copy(t).wait_recv()
        for q, d in zip(own, (2, 1, 3)):
            QS[d - 1, g] = all_rows(q, (x + d) % 4, g).astype(BF16)
            qx_copy(g, d).start()
        Q[g] = all_rows(own_rows(x, g), x, g)
    for g in range(2):
        for d in (1, 3, 2):
            qx_copy(g, d).wait_recv()
        total = Q[g] + QR[0, g].astype(F32) + QR[2, g].astype(F32) + QR[1, g].astype(F32)
        R[4 * g : 4 * g + 4] = total
        RS[4 * g : 4 * g + 4] = total.astype(BF16)
        for to in range(4 * g, 4 * g + 4):
            @pl.when(l != to)
            def _():
                rz_copy(to).start()

    grad_out[...] = R[l]

    @pl.loop(1, 8)
    def _(k):
        rz_wait((l + k) % 8)
        grad_out[...] += RR[(l + k) % 8].astype(F32)

    def drain_gather():
        for t in range(2):
            g0_copy(t).wait_send()
            for q in range(2):
                z_copy(t, z, q).wait_send()

            for k in range(1, 8):
                o = origin(k)
                if t == 0:
                    g_copy(o).wait_send()

                def left():
                    for q in range(2):
                        z_copy(t, o, q).wait_send()

                if k < 7:
                    left()
                else:
                    pl.when(c == t)(left)

            @pl.when(c == t)
            def _():
                g_far(t).wait_send()

            for d in range(1, 4):
                wx_copy(d, t).wait_send()
                wy_copy(d, t).wait_send()

    def drain_partials():
        for t in range(2):
            for hh in range(2):
                for d in range(1, 4):
                    xr_copy(t, hh, d).wait_send()

    def drain_proj():
        for t in range(2):
            for hh in range(2):
                for d in range(1, 4):
                    y_copy(t, hh, d).wait_send()
            for hh in range(2):
                pb_copy(t, hh).wait_send()
            k_copy(t).wait_send()

    drain_gather()
    drain_partials()
    drain_proj()
    for g in range(2):
        for d in range(1, 4):
            qx_copy(g, d).wait_send()

    @pl.loop(1, 8)
    def _(k):
        rz_copy((l + k) % 8).wait_send()


def hand_over(coef_in, grad_in, coef_out, grad_out):
    coef_out[...] = coef_in[...]
    grad_out[...] = grad_in[...]


def on_device(obs, cot, cell_basis, cycle_basis, cell_spectrum, cycle_spectrum, noise_var):
    vmem = pl.BlockSpec(memory_space=pltpu.VMEM)
    dma = pltpu.SemaphoreType.DMA
    coefficients, basis_grad = pl.pallas_call(
        kernel,
        out_shape=(
            jax.ShapeDtypeStruct((256, 128), BF16),
            jax.ShapeDtypeStruct((32, 256), F32),
        ),
        in_specs=[pl.BlockSpec(memory_space=pltpu.HBM)] * 7,
        out_specs=(vmem, vmem),
        scratch_shapes=[
            pltpu.VMEM((16, 2, 2, 256, 128), BF16),
            pltpu.VMEM((8, 2, 128, 512), BF16),
            pltpu.VMEM((2, 2, 256, 512), F32),
            pltpu.VMEM((2, 3, 2, 256, 128), BF16),
            pltpu.VMEM((2, 3, 2, 256, 128), BF16),
            pltpu.VMEM((2, 2, 4, 4, 2, 32, 128), BF16),
            pltpu.VMEM((2, 2, 4, 4, 32, 128), BF16),
            pltpu.VMEM((8, 256, 256), BF16),
            pltpu.VMEM((8, 256, 256), BF16),
            pltpu.VMEM((1, 128), F32),
            pltpu.VMEM((1, 256), F32),
            pltpu.SMEM((1,), F32),
            pltpu.VMEM((256, 128), F32),
            pltpu.VMEM((2, 256, 128), BF16),
            pltpu.VMEM((2, 256, 128), BF16),
            pltpu.VMEM((2, 4, 32, 256), F32),
            pltpu.VMEM((3, 2, 4, 32, 256), BF16),
            pltpu.VMEM((3, 2, 4, 32, 256), BF16),
            pltpu.VMEM((8, 32, 256), F32),
            pltpu.VMEM((8, 32, 256), BF16),
            pltpu.VMEM((8, 32, 256), BF16),
            dma((7,)),
            dma((2, 2)),
            dma((2, 16, 2)), dma((2, 16, 2)),
            dma((16,)), dma((16,)),
            dma((3, 2)), dma((3, 2)),
            dma((3, 2)), dma((3, 2)),
            dma((2, 2, 3)), dma((2, 2, 3)),
            dma((2, 2, 3)), dma((2, 2, 3)),
            dma((2, 2, 2)), dma((2, 2)),
            dma((2, 3)), dma((2, 3)),
            dma((8,)), dma((8,)),
        ],
        compiler_params=pltpu.CompilerParams(
            collective_id=0, has_side_effects=True, vmem_limit_bytes=60 << 20
        ),
    )(
        obs,
        cot,
        cell_basis.reshape(8, 4, 2, 128, 128),
        cycle_basis.reshape(8, 256, 256),
        cell_spectrum.reshape(1, 128),
        cycle_spectrum.reshape(1, 256),
        noise_var,
    )
    return pl.pallas_call(
        hand_over,
        out_shape=(
            jax.ShapeDtypeStruct((256, 128), BF16),
            jax.ShapeDtypeStruct((32, 256), F32),
        ),
        in_specs=[vmem] * 2,
        out_specs=(vmem, vmem),
    )(coefficients, basis_grad)


def solution(mesh):
    in_specs = (
        P("narrow", "wide"),
        P("narrow", "wide"),
        P(None, "wide"),
        P(None, "narrow"),
        P("wide"),
        P("narrow"),
        P(),
    )
    out_specs = (P("narrow", "wide"), P("wide", "narrow"))
    return jax.shard_map(
        on_device, mesh=mesh, in_specs=in_specs, out_specs=out_specs, check_vma=False
    )
```

```python
import jax
import jax.numpy as jnp
from jax import lax
from jax.experimental import pallas as pl
from jax.experimental.pallas import tpu as pltpu
from jax.sharding import PartitionSpec as P

F32 = jnp.float32
BF16 = jnp.bfloat16
MESH = pl.DeviceIdType.MESH


def dot_nt(left, right):
    return lax.dot_general(left, right, (((1,), (1,)), ((), ())), preferred_element_type=F32)


def dot_nn(left, right):
    return lax.dot_general(left, right, (((1,), (0,)), ((), ())), preferred_element_type=F32)


def kernel(
    obs, cot, cb, cyc, cell_row, cyc_row, noise,
    coef_out, grad_out,
    G, W, acc, XS, XR, PF, PB, cycV, CT, cellV, cycrV, noiseS, spec, KO, KS,
    Q, QS, QR, R, RS, RR,
    in_sem, g0_sem, z_send, z_recv, g_send, g_recv,
    wx_send, wx_recv, wy_send, wy_recv, xr_send, xr_recv,
    y_send, y_recv, pb_sem, k_sem, qx_send, qx_recv, rz_send, rz_recv,
):
    w = lax.axis_index("wide")
    n = lax.axis_index("narrow")
    l, x, c = w // 8, (w // 2) % 4, w % 2
    h, y = n // 4, n % 4
    z = h * 8 + l
    s = 1 - 2 * c

    def wide(l_, x_, c_):
        return {"wide": (l_ * 4 + x_) * 2 + c_}

    def narrow(h_, y_):
        return {"narrow": h_ * 4 + y_}

    def along_z(z_):
        return {"wide": ((z_ % 8) * 4 + x) * 2 + c, "narrow": (z_ // 8) * 4 + y}

    sib = wide(l, x, 1 - c)

    def rcopy(src, dst, ss, rs, dev):
        return pltpu.make_async_remote_copy(
            src_ref=src, dst_ref=dst, send_sem=ss, recv_sem=rs, device_id=dev, device_id_type=MESH
        )

    bar = pltpu.get_barrier_semaphore()

    def greet(dev):
        pl.semaphore_signal(bar, inc=1, device_id=dev, device_id_type=MESH)

    for d in (2, 1, 3):
        greet(wide(l, (x + d) % 4, c))
        greet(narrow(h, (y + d) % 4))
    greet(along_z((z - s + 16) % 16))
    greet(sib)

    loads = [
        pltpu.make_async_copy(obs, G.at[z, 0, c], in_sem.at[0]),
        pltpu.make_async_copy(cot, G.at[z, 1, c], in_sem.at[1]),
        pltpu.make_async_copy(cb.at[:, x], W.at[:, :, :, pl.ds(0, 128)], in_sem.at[2]),
        pltpu.make_async_copy(cyc, cycV, in_sem.at[3]),
        pltpu.make_async_copy(cell_row, cellV, in_sem.at[4]),
        pltpu.make_async_copy(cyc_row, cycrV, in_sem.at[5]),
        pltpu.make_async_copy(noise, noiseS, in_sem.at[6]),
    ]
    for load in loads:
        load.start()
    loads[0].wait()
    loads[1].wait()
    pl.semaphore_wait(bar, 8)

    def z_copy(t, o, q):
        part = G.at[o, t, q]
        return rcopy(
            part, part, z_send.at[t, o, q], z_recv.at[t, o, q], along_z((z + s + 16) % 16)
        )

    def g0_copy(t):
        return rcopy(G.at[z, t, c], G.at[z, t, c], g0_sem.at[t, 0], g0_sem.at[t, 1], sib)

    def g0_wait(t):
        part = G.at[z, t, 1 - c]
        rcopy(part, part, g0_sem.at[t, 0], g0_sem.at[t, 1], sib).wait_recv()

    def g_copy(o):
        return rcopy(G.at[o], G.at[o], g_send.at[o], g_recv.at[o], sib)

    def g_far(t):
        far = (z + 8) % 16
        return rcopy(G.at[far, t], G.at[far, t], g_send.at[far], g_recv.at[far], sib)

    def origin(k):
        return (z - s * k + 16) % 16

    def z_step(t, k):
        def go():
            o = origin(k)
            for q in (c, 1 - c):
                z_copy(t, o, q).wait_recv()

                def send():
                    z_copy(t, o, q).start()

                if k < 7:
                    send()
                elif k == 7:
                    pl.when(c == t)(send)

            if k == 8:
                g_far(t).start()

        if k < 8:
            go()
        else:
            pl.when(c == t)(go)

    def wx_copy(d, p):
        q = (y + 2 * p) % 4
        to = (x + d) % 4
        return rcopy(
            cb.at[pl.ds(2 * q, 2), to],
            W.at[pl.ds(2 * q, 2), :, :, pl.ds(128 * (4 - d), 128)],
            wx_send.at[d - 1, p], wx_recv.at[d - 1, p], wide(l, to, c),
        )

    def wx_wait(d, p):
        q = (y + 2 * p) % 4
        part = W.at[pl.ds(2 * q, 2), :, :, pl.ds(128 * (4 - d), 128)]
        rcopy(part, part, wx_send.at[d - 1, p], wx_recv.at[d - 1, p], sib).wait_recv()

    def wy_copy(d, up):
        part = W.at[pl.ds(2 * y, 2), :, :, pl.ds(128 * (4 - d), 128)]
        return rcopy(
            part, part, wy_send.at[d - 1, up], wy_recv.at[d - 1, up],
            narrow(h, (y + 2 * up + 3) % 4),
        )

    def wy_wait(d, up):
        q = (y + 5 - 2 * up) % 4
        part = W.at[pl.ds(2 * q, 2), :, :, pl.ds(128 * (4 - d), 128)]
        rcopy(part, part, wy_send.at[d - 1, up], wy_recv.at[d - 1, up], sib).wait_recv()

    def w_step(d):
        wx_wait(d, 0)
        wy_copy(d, 1).start()
        wy_copy(d, 0).start()

    for t in range(2):
        z_copy(t, z, c).start()
        g0_copy(t).start()
    for t in range(2):
        g0_wait(t)
        z_copy(t, z, 1 - c).start()
    for p in range(2):
        for d in (1, 3, 2):
            wx_copy(d, p).start()

    acc[...] = jnp.zeros_like(acc)
    for i in range(3, 7):
        loads[i].wait()

    def transpose(i):
        CT[i] = cycV[i].T

    def mac(t, o):
        block = jnp.concatenate([G[o, t, 0], G[o, t, 1]], axis=1)
        acc[o // 8, t] += dot_nn(block, W[o % 8].reshape(256, 512))

    def mac_both(o):
        block = jnp.concatenate(
            [G[o, :, 0].reshape(512, 128), G[o, :, 1].reshape(512, 128)], axis=1
        )
        part = dot_nn(block, W[o % 8].reshape(256, 512))
        acc[o // 8] += part.reshape(2, 256, 512)

    def macs(k):
        mac_both(origin(k))
        other = (z + s * k + 16) % 16
        g_copy(other).wait_recv()
        mac_both(other)

    def last_mac(t):
        z_step(t, 8)

        @pl.when(c != t)
        def _():
            g_far(t).wait_recv()

        mac(t, (z + 8) % 16)

    def xr_copy(t, hh, d):
        return rcopy(
            XS.at[t, d - 1, hh], XR.at[t, d - 1, hh],
            xr_send.at[t, hh, d - 1], xr_recv.at[t, hh, d - 1], wide(l, (x + d) % 4, c),
        )

    def send_partials(t, hh):
        for d in (2, 1, 3):
            XS[t, d - 1, hh] = acc[hh, t, :, 128 * d : 128 * d + 128].astype(BF16)
            xr_copy(t, hh, d).start()

    def z_steps(k):
        z_step(0, k)
        z_step(1, k)
        g_copy(origin(k)).start()

    z_steps(1)
    w_step(1)
    w_step(3)
    z_steps(2)
    w_step(2)
    for i in range(4):
        transpose(i)
    z_steps(3)
    for i in range(4, 8):
        transpose(i)
    spec[...] = jnp.broadcast_to(cycrV[...], (128, 256)).T * cellV[...] + noiseS[0]
    z_steps(4)
    loads[2].wait()
    for d in (1, 3, 2):
        wx_wait(d, 1)
        wy_wait(d, 0)
        wy_wait(d, 1)
    mac_both(z)
    macs(1)
    for k in (5, 6, 7):
        z_steps(k)
        for j in ((2, 3), (4, 5), (6, 7))[k - 5]:
            macs(j)
    for t in range(2):
        send_partials(t, h)
    for t in range(2):
        last_mac(t)
        send_partials(t, 1 - h)

    def y_copy(t, hh, d):
        rows_of = PF.at[t, hh, y]
        return rcopy(
            rows_of, rows_of, y_send.at[t, hh, d - 1], y_recv.at[t, hh, d - 1],
            narrow(h, (y + d) % 4),
        )

    def y_wait(t, hh, d):
        rows_of = PF.at[t, hh, (y + 4 - d) % 4]
        rcopy(rows_of, rows_of, y_send.at[t, hh, d - 1], y_recv.at[t, hh, d - 1], sib).wait_recv()

    def finish_proj(t, hh):
        total = acc[hh, t, :, :128]
        for d in (1, 3, 2):
            xr_copy(t, hh, d).wait_recv()
            total = total + XR[t, d - 1, hh].astype(F32)
        PF[t, hh, y] = total.astype(BF16).reshape(4, 2, 32, 128)
        for d in (2, 1, 3):
            y_copy(t, hh, d).start()

    def pb_copy(t, hh):
        return rcopy(
            PF.at[t, hh, :, :, 1 - c], PB.at[t, hh], pb_sem.at[t, hh, 0], pb_sem.at[t, hh, 1], sib
        )

    def k_copy(t):
        return rcopy(KO.at[t], KS.at[t], k_sem.at[t, 0], k_sem.at[t, 1], sib)

    def rotate(t):
        rot = jnp.zeros((256, 128), F32)
        for hh in (h, 1 - h):
            for d in (1, 3, 2):
                y_wait(t, hh, d)
            pb_copy(t, hh).start()
            for yy in range(4):
                rot = rot + dot_nn(CT[4 * hh + yy], PF[t, hh, yy].reshape(256, 128))
        KO[t] = (rot / spec[...]).astype(BF16)
        k_copy(t).start()

    for hh in (h, 1 - h):
        for t in range(2):
            finish_proj(t, hh)
    rotate(0)
    coef_out[...] = KO[0]
    rotate(1)

    def own_rows(xx, g):
        q = dot_nt(PF[1, g, :, xx, c].reshape(128, 128), KO[0])
        return q + dot_nt(PF[0, g, :, xx, c].reshape(128, 128), KO[1])

    def all_rows(q, xx, g):
        q = q + dot_nt(PB[1, g, :, xx].reshape(128, 128), KS[0])
        q = q + dot_nt(PB[0, g, :, xx].reshape(128, 128), KS[1])
        return q.reshape(4, 32, 256)

    def qx_copy(g, d):
        return rcopy(
            QS.at[d - 1, g], QR.at[d - 1, g], qx_send.at[g, d - 1], qx_recv.at[g, d - 1],
            wide(l, (x + d) % 4, c),
        )

    def rz_copy(to):
        return rcopy(RS.at[to], RR.at[l], rz_send.at[to], rz_recv.at[l], wide(to, x, c))

    def rz_wait(frm):
        rcopy(
            RR.at[frm], RR.at[frm], rz_send.at[frm], rz_recv.at[frm], wide(frm, x, c)
        ).wait_recv()

    for g in range(2):
        own = [own_rows((x + d) % 4, g) for d in (2, 1, 3)]
        if g == 0:
            for t in range(2):
                for hh in range(2):
                    pb_copy(t, hh).wait_recv()
                k_copy(t).wait_recv()
        for q, d in zip(own, (2, 1, 3)):
            QS[d - 1, g] = all_rows(q, (x + d) % 4, g).astype(BF16)
            qx_copy(g, d).start()
        Q[g] = all_rows(own_rows(x, g), x, g)
    for g in range(2):
        for d in (1, 3, 2):
            qx_copy(g, d).wait_recv()
        total = Q[g] + QR[0, g].astype(F32) + QR[2, g].astype(F32) + QR[1, g].astype(F32)
        R[4 * g : 4 * g + 4] = total
        RS[4 * g : 4 * g + 4] = total.astype(BF16)
        for to in range(4 * g, 4 * g + 4):
            @pl.when(l != to)
            def _():
                rz_copy(to).start()

    grad_out[...] = R[l]

    @pl.loop(1, 8)
    def _(k):
        rz_wait((l + k) % 8)
        grad_out[...] += RR[(l + k) % 8].astype(F32)

    def drain_gather():
        for t in range(2):
            g0_copy(t).wait_send()
            for q in range(2):
                z_copy(t, z, q).wait_send()

            for k in range(1, 8):
                o = origin(k)
                if t == 0:
                    g_copy(o).wait_send()

                def left():
                    for q in range(2):
                        z_copy(t, o, q).wait_send()

                if k < 7:
                    left()
                else:
                    pl.when(c == t)(left)

            @pl.when(c == t)
            def _():
                g_far(t).wait_send()

            for d in range(1, 4):
                wx_copy(d, t).wait_send()
                wy_copy(d, t).wait_send()

    def drain_partials():
        for t in range(2):
            for hh in range(2):
                for d in range(1, 4):
                    xr_copy(t, hh, d).wait_send()

    def drain_proj():
        for t in range(2):
            for hh in range(2):
                for d in range(1, 4):
                    y_copy(t, hh, d).wait_send()
            for hh in range(2):
                pb_copy(t, hh).wait_send()
            k_copy(t).wait_send()

    drain_gather()
    drain_partials()
    drain_proj()
    for g in range(2):
        for d in range(1, 4):
            qx_copy(g, d).wait_send()

    @pl.loop(1, 8)
    def _(k):
        rz_copy((l + k) % 8).wait_send()


def hand_over(coef_in, grad_in, coef_out, grad_out):
    coef_out[...] = coef_in[...]
    grad_out[...] = grad_in[...]


def on_device(obs, cot, cell_basis, cycle_basis, cell_spectrum, cycle_spectrum, noise_var):
    vmem = pl.BlockSpec(memory_space=pltpu.VMEM)
    dma = pltpu.SemaphoreType.DMA
    coefficients, basis_grad = pl.pallas_call(
        kernel,
        out_shape=(
            jax.ShapeDtypeStruct((256, 128), BF16),
            jax.ShapeDtypeStruct((32, 256), F32),
        ),
        in_specs=[pl.BlockSpec(memory_space=pltpu.HBM)] * 7,
        out_specs=(vmem, vmem),
        scratch_shapes=[
            pltpu.VMEM((16, 2, 2, 256, 128), BF16),
            pltpu.VMEM((8, 2, 128, 512), BF16),
            pltpu.VMEM((2, 2, 256, 512), F32),
            pltpu.VMEM((2, 3, 2, 256, 128), BF16),
            pltpu.VMEM((2, 3, 2, 256, 128), BF16),
            pltpu.VMEM((2, 2, 4, 4, 2, 32, 128), BF16),
            pltpu.VMEM((2, 2, 4, 4, 32, 128), BF16),
            pltpu.VMEM((8, 256, 256), BF16),
            pltpu.VMEM((8, 256, 256), BF16),
            pltpu.VMEM((1, 128), F32),
            pltpu.VMEM((1, 256), F32),
            pltpu.SMEM((1,), F32),
            pltpu.VMEM((256, 128), F32),
            pltpu.VMEM((2, 256, 128), BF16),
            pltpu.VMEM((2, 256, 128), BF16),
            pltpu.VMEM((2, 4, 32, 256), F32),
            pltpu.VMEM((3, 2, 4, 32, 256), BF16),
            pltpu.VMEM((3, 2, 4, 32, 256), BF16),
            pltpu.VMEM((8, 32, 256), F32),
            pltpu.VMEM((8, 32, 256), BF16),
            pltpu.VMEM((8, 32, 256), BF16),
            dma((7,)),
            dma((2, 2)),
            dma((2, 16, 2)), dma((2, 16, 2)),
            dma((16,)), dma((16,)),
            dma((3, 2)), dma((3, 2)),
            dma((3, 2)), dma((3, 2)),
            dma((2, 2, 3)), dma((2, 2, 3)),
            dma((2, 2, 3)), dma((2, 2, 3)),
            dma((2, 2, 2)), dma((2, 2)),
            dma((2, 3)), dma((2, 3)),
            dma((8,)), dma((8,)),
        ],
        compiler_params=pltpu.CompilerParams(
            collective_id=0, has_side_effects=True, vmem_limit_bytes=60 << 20
        ),
    )(
        obs,
        cot,
        cell_basis.reshape(8, 4, 2, 128, 128),
        cycle_basis.reshape(8, 256, 256),
        cell_spectrum.reshape(1, 128),
        cycle_spectrum.reshape(1, 256),
        noise_var,
    )
    return pl.pallas_call(
        hand_over,
        out_shape=(
            jax.ShapeDtypeStruct((256, 128), BF16),
            jax.ShapeDtypeStruct((32, 256), F32),
        ),
        in_specs=[vmem] * 2,
        out_specs=(vmem, vmem),
    )(coefficients, basis_grad)


def solution(mesh):
    in_specs = (
        P("narrow", "wide"),
        P("narrow", "wide"),
        P(None, "wide"),
        P(None, "narrow"),
        P("wide"),
        P("narrow"),
        P(),
    )
    out_specs = (P("narrow", "wide"), P("wide", "narrow"))
    return jax.shard_map(
        on_device, mesh=mesh, in_specs=in_specs, out_specs=out_specs, check_vma=False
    )
```

```python
import jax
import jax.numpy as jnp
from jax import lax
from jax.experimental import pallas as pl
from jax.experimental.pallas import tpu as pltpu
from jax.sharding import PartitionSpec as P

F32 = jnp.float32
BF16 = jnp.bfloat16
MESH = pl.DeviceIdType.MESH


def dot_nt(left, right):
    return lax.dot_general(left, right, (((1,), (1,)), ((), ())), preferred_element_type=F32)


def dot_nn(left, right):
    return lax.dot_general(left, right, (((1,), (0,)), ((), ())), preferred_element_type=F32)


def kernel(
    obs, cot, cb, cyc, cell_row, cyc_row, noise,
    coef_out, grad_out,
    G, W, acc, XS, XR, PF, PB, cycV, CT, cellV, cycrV, noiseS, spec, KO, KS,
    Q, QS, QR, R, RS, RR,
    in_sem, g0_sem, z_send, z_recv, g_send, g_recv,
    wx_send, wx_recv, wy_send, wy_recv, xr_send, xr_recv,
    y_send, y_recv, pb_sem, k_sem, qx_send, qx_recv, rz_send, rz_recv,
):
    w = lax.axis_index("wide")
    n = lax.axis_index("narrow")
    l, x, c = w // 8, (w // 2) % 4, w % 2
    h, y = n // 4, n % 4
    z = h * 8 + l
    s = 1 - 2 * c

    def wide(l_, x_, c_):
        return {"wide": (l_ * 4 + x_) * 2 + c_}

    def narrow(h_, y_):
        return {"narrow": h_ * 4 + y_}

    def along_z(z_):
        return {"wide": ((z_ % 8) * 4 + x) * 2 + c, "narrow": (z_ // 8) * 4 + y}

    sib = wide(l, x, 1 - c)

    def rcopy(src, dst, ss, rs, dev):
        return pltpu.make_async_remote_copy(
            src_ref=src, dst_ref=dst, send_sem=ss, recv_sem=rs, device_id=dev, device_id_type=MESH
        )

    bar = pltpu.get_barrier_semaphore()

    def greet(dev):
        pl.semaphore_signal(bar, inc=1, device_id=dev, device_id_type=MESH)

    for d in (2, 1, 3):
        greet(wide(l, (x + d) % 4, c))
        greet(narrow(h, (y + d) % 4))
    greet(along_z((z - s + 16) % 16))
    greet(sib)

    loads = [
        pltpu.make_async_copy(obs, G.at[z, 0, c], in_sem.at[0]),
        pltpu.make_async_copy(cot, G.at[z, 1, c], in_sem.at[1]),
        pltpu.make_async_copy(cb.at[:, x], W.at[:, :, :, pl.ds(0, 128)], in_sem.at[2]),
        pltpu.make_async_copy(cyc, cycV, in_sem.at[3]),
        pltpu.make_async_copy(cell_row, cellV, in_sem.at[4]),
        pltpu.make_async_copy(cyc_row, cycrV, in_sem.at[5]),
        pltpu.make_async_copy(noise, noiseS, in_sem.at[6]),
    ]
    for load in loads:
        load.start()
    loads[0].wait()
    loads[1].wait()
    pl.semaphore_wait(bar, 8)

    def z_copy(t, o, q):
        part = G.at[o, t, q]
        return rcopy(
            part, part, z_send.at[t, o, q], z_recv.at[t, o, q], along_z((z + s + 16) % 16)
        )

    def g0_copy(t):
        return rcopy(G.at[z, t, c], G.at[z, t, c], g0_sem.at[t, 0], g0_sem.at[t, 1], sib)

    def g0_wait(t):
        part = G.at[z, t, 1 - c]
        rcopy(part, part, g0_sem.at[t, 0], g0_sem.at[t, 1], sib).wait_recv()

    def g_copy(o):
        return rcopy(G.at[o], G.at[o], g_send.at[o], g_recv.at[o], sib)

    def g_far(t):
        far = (z + 8) % 16
        return rcopy(G.at[far, t], G.at[far, t], g_send.at[far], g_recv.at[far], sib)

    def origin(k):
        return (z - s * k + 16) % 16

    def z_step(t, k):
        def go():
            o = origin(k)
            for q in (c, 1 - c):
                z_copy(t, o, q).wait_recv()

                def send():
                    z_copy(t, o, q).start()

                if k < 7:
                    send()
                elif k == 7:
                    pl.when(c == t)(send)

            if k == 8:
                g_far(t).start()

        if k < 8:
            go()
        else:
            pl.when(c == t)(go)

    def wx_copy(d, p):
        q = (y + 2 * p) % 4
        to = (x + d) % 4
        return rcopy(
            cb.at[pl.ds(2 * q, 2), to],
            W.at[pl.ds(2 * q, 2), :, :, pl.ds(128 * (4 - d), 128)],
            wx_send.at[d - 1, p], wx_recv.at[d - 1, p], wide(l, to, c),
        )

    def wx_wait(d, p):
        q = (y + 2 * p) % 4
        part = W.at[pl.ds(2 * q, 2), :, :, pl.ds(128 * (4 - d), 128)]
        rcopy(part, part, wx_send.at[d - 1, p], wx_recv.at[d - 1, p], sib).wait_recv()

    def wy_copy(d, up):
        part = W.at[pl.ds(2 * y, 2), :, :, pl.ds(128 * (4 - d), 128)]
        return rcopy(
            part, part, wy_send.at[d - 1, up], wy_recv.at[d - 1, up],
            narrow(h, (y + 2 * up + 3) % 4),
        )

    def wy_wait(d, up):
        q = (y + 5 - 2 * up) % 4
        part = W.at[pl.ds(2 * q, 2), :, :, pl.ds(128 * (4 - d), 128)]
        rcopy(part, part, wy_send.at[d - 1, up], wy_recv.at[d - 1, up], sib).wait_recv()

    def w_step(d):
        wx_wait(d, 0)
        wy_copy(d, 1).start()
        wy_copy(d, 0).start()

    for t in range(2):
        z_copy(t, z, c).start()
        g0_copy(t).start()
    for t in range(2):
        g0_wait(t)
        z_copy(t, z, 1 - c).start()
    for p in range(2):
        for d in (1, 3, 2):
            wx_copy(d, p).start()

    acc[...] = jnp.zeros_like(acc)
    for i in range(3, 7):
        loads[i].wait()

    def transpose(i):
        CT[i] = cycV[i].T

    def mac(t, o):
        block = jnp.concatenate([G[o, t, 0], G[o, t, 1]], axis=1)
        acc[o // 8, t] += dot_nn(block, W[o % 8].reshape(256, 512))

    def mac_both(o):
        block = jnp.concatenate(
            [G[o, :, 0].reshape(512, 128), G[o, :, 1].reshape(512, 128)], axis=1
        )
        part = dot_nn(block, W[o % 8].reshape(256, 512))
        acc[o // 8] += part.reshape(2, 256, 512)

    def macs(k):
        mac_both(origin(k))
        other = (z + s * k + 16) % 16
        g_copy(other).wait_recv()
        mac_both(other)

    def last_mac(t):
        z_step(t, 8)

        @pl.when(c != t)
        def _():
            g_far(t).wait_recv()

        mac(t, (z + 8) % 16)

    def xr_copy(t, hh, d):
        return rcopy(
            XS.at[t, d - 1, hh], XR.at[t, d - 1, hh],
            xr_send.at[t, hh, d - 1], xr_recv.at[t, hh, d - 1], wide(l, (x + d) % 4, c),
        )

    def send_partials(t, hh):
        for d in (2, 1, 3):
            XS[t, d - 1, hh] = acc[hh, t, :, 128 * d : 128 * d + 128].astype(BF16)
            xr_copy(t, hh, d).start()

    def z_steps(k):
        z_step(0, k)
        z_step(1, k)
        g_copy(origin(k)).start()

    z_steps(1)
    w_step(1)
    w_step(3)
    z_steps(2)
    w_step(2)
    for i in range(4):
        transpose(i)
    z_steps(3)
    for i in range(4, 8):
        transpose(i)
    spec[...] = jnp.broadcast_to(cycrV[...], (128, 256)).T * cellV[...] + noiseS[0]
    z_steps(4)
    loads[2].wait()
    for d in (1, 3, 2):
        wx_wait(d, 1)
        wy_wait(d, 0)
        wy_wait(d, 1)
    mac_both(z)
    macs(1)
    for k in (5, 6, 7):
        z_steps(k)
        for j in ((2, 3), (4, 5), (6, 7))[k - 5]:
            macs(j)
    for t in range(2):
        send_partials(t, h)
    for t in range(2):
        last_mac(t)
        send_partials(t, 1 - h)

    def y_copy(t, hh, d):
        rows_of = PF.at[t, hh, y]
        return rcopy(
            rows_of, rows_of, y_send.at[t, hh, d - 1], y_recv.at[t, hh, d - 1],
            narrow(h, (y + d) % 4),
        )

    def y_wait(t, hh, d):
        rows_of = PF.at[t, hh, (y + 4 - d) % 4]
        rcopy(rows_of, rows_of, y_send.at[t, hh, d - 1], y_recv.at[t, hh, d - 1], sib).wait_recv()

    def finish_proj(t, hh):
        total = acc[hh, t, :, :128]
        for d in (1, 3, 2):
            xr_copy(t, hh, d).wait_recv()
            total = total + XR[t, d - 1, hh].astype(F32)
        PF[t, hh, y] = total.astype(BF16).reshape(4, 2, 32, 128)
        for d in (2, 1, 3):
            y_copy(t, hh, d).start()

    def pb_copy(t, hh):
        return rcopy(
            PF.at[t, hh, :, :, 1 - c], PB.at[t, hh], pb_sem.at[t, hh, 0], pb_sem.at[t, hh, 1], sib
        )

    def k_copy(t):
        return rcopy(KO.at[t], KS.at[t], k_sem.at[t, 0], k_sem.at[t, 1], sib)

    def rotate(t):
        rot = jnp.zeros((256, 128), F32)
        for hh in (h, 1 - h):
            for d in (1, 3, 2):
                y_wait(t, hh, d)
            pb_copy(t, hh).start()
            for yy in range(4):
                rot = rot + dot_nn(CT[4 * hh + yy], PF[t, hh, yy].reshape(256, 128))
        KO[t] = (rot / spec[...]).astype(BF16)
        k_copy(t).start()

    for hh in (h, 1 - h):
        for t in range(2):
            finish_proj(t, hh)
    rotate(0)
    coef_out[...] = KO[0]
    rotate(1)

    def own_rows(xx, g):
        q = dot_nt(PF[1, g, :, xx, c].reshape(128, 128), KO[0])
        return q + dot_nt(PF[0, g, :, xx, c].reshape(128, 128), KO[1])

    def all_rows(q, xx, g):
        q = q + dot_nt(PB[1, g, :, xx].reshape(128, 128), KS[0])
        q = q + dot_nt(PB[0, g, :, xx].reshape(128, 128), KS[1])
        return q.reshape(4, 32, 256)

    def qx_copy(g, d):
        return rcopy(
            QS.at[d - 1, g], QR.at[d - 1, g], qx_send.at[g, d - 1], qx_recv.at[g, d - 1],
            wide(l, (x + d) % 4, c),
        )

    def rz_copy(to):
        return rcopy(RS.at[to], RR.at[l], rz_send.at[to], rz_recv.at[l], wide(to, x, c))

    def rz_wait(frm):
        rcopy(
            RR.at[frm], RR.at[frm], rz_send.at[frm], rz_recv.at[frm], wide(frm, x, c)
        ).wait_recv()

    halves = (1 - l // 4, l // 4)
    for g in halves:
        own = [own_rows((x + d) % 4, g) for d in (2, 1, 3)]
        if g is halves[0]:
            for t in range(2):
                for hh in range(2):
                    pb_copy(t, hh).wait_recv()
                k_copy(t).wait_recv()
        for q, d in zip(own, (2, 1, 3)):
            QS[d - 1, g] = all_rows(q, (x + d) % 4, g).astype(BF16)
            qx_copy(g, d).start()
        Q[g] = all_rows(own_rows(x, g), x, g)
    for g in halves:
        for d in (1, 3, 2):
            qx_copy(g, d).wait_recv()
        total = Q[g] + QR[0, g].astype(F32) + QR[2, g].astype(F32) + QR[1, g].astype(F32)
        R[pl.ds(4 * g, 4)] = total
        RS[pl.ds(4 * g, 4)] = total.astype(BF16)
        for to in [4 * g + i for i in range(4)]:
            @pl.when(l != to)
            def _():
                rz_copy(to).start()

    grad_out[...] = R[l]

    @pl.loop(1, 8)
    def _(k):
        rz_wait((l + k) % 8)
        grad_out[...] += RR[(l + k) % 8].astype(F32)

    def drain_gather():
        for t in range(2):
            g0_copy(t).wait_send()
            for q in range(2):
                z_copy(t, z, q).wait_send()

            for k in range(1, 8):
                o = origin(k)
                if t == 0:
                    g_copy(o).wait_send()

                def left():
                    for q in range(2):
                        z_copy(t, o, q).wait_send()

                if k < 7:
                    left()
                else:
                    pl.when(c == t)(left)

            @pl.when(c == t)
            def _():
                g_far(t).wait_send()

            for d in range(1, 4):
                wx_copy(d, t).wait_send()
                wy_copy(d, t).wait_send()

    def drain_partials():
        for t in range(2):
            for hh in range(2):
                for d in range(1, 4):
                    xr_copy(t, hh, d).wait_send()

    def drain_proj():
        for t in range(2):
            for hh in range(2):
                for d in range(1, 4):
                    y_copy(t, hh, d).wait_send()
            for hh in range(2):
                pb_copy(t, hh).wait_send()
            k_copy(t).wait_send()

    drain_gather()
    drain_partials()
    drain_proj()
    for g in range(2):
        for d in range(1, 4):
            qx_copy(g, d).wait_send()

    @pl.loop(1, 8)
    def _(k):
        rz_copy((l + k) % 8).wait_send()


def hand_over(coef_in, grad_in, coef_out, grad_out):
    coef_out[...] = coef_in[...]
    grad_out[...] = grad_in[...]


def on_device(obs, cot, cell_basis, cycle_basis, cell_spectrum, cycle_spectrum, noise_var):
    vmem = pl.BlockSpec(memory_space=pltpu.VMEM)
    dma = pltpu.SemaphoreType.DMA
    coefficients, basis_grad = pl.pallas_call(
        kernel,
        out_shape=(
            jax.ShapeDtypeStruct((256, 128), BF16),
            jax.ShapeDtypeStruct((32, 256), F32),
        ),
        in_specs=[pl.BlockSpec(memory_space=pltpu.HBM)] * 7,
        out_specs=(vmem, vmem),
        scratch_shapes=[
            pltpu.VMEM((16, 2, 2, 256, 128), BF16),
            pltpu.VMEM((8, 2, 128, 512), BF16),
            pltpu.VMEM((2, 2, 256, 512), F32),
            pltpu.VMEM((2, 3, 2, 256, 128), BF16),
            pltpu.VMEM((2, 3, 2, 256, 128), BF16),
            pltpu.VMEM((2, 2, 4, 4, 2, 32, 128), BF16),
            pltpu.VMEM((2, 2, 4, 4, 32, 128), BF16),
            pltpu.VMEM((8, 256, 256), BF16),
            pltpu.VMEM((8, 256, 256), BF16),
            pltpu.VMEM((1, 128), F32),
            pltpu.VMEM((1, 256), F32),
            pltpu.SMEM((1,), F32),
            pltpu.VMEM((256, 128), F32),
            pltpu.VMEM((2, 256, 128), BF16),
            pltpu.VMEM((2, 256, 128), BF16),
            pltpu.VMEM((2, 4, 32, 256), F32),
            pltpu.VMEM((3, 2, 4, 32, 256), BF16),
            pltpu.VMEM((3, 2, 4, 32, 256), BF16),
            pltpu.VMEM((8, 32, 256), F32),
            pltpu.VMEM((8, 32, 256), BF16),
            pltpu.VMEM((8, 32, 256), BF16),
            dma((7,)),
            dma((2, 2)),
            dma((2, 16, 2)), dma((2, 16, 2)),
            dma((16,)), dma((16,)),
            dma((3, 2)), dma((3, 2)),
            dma((3, 2)), dma((3, 2)),
            dma((2, 2, 3)), dma((2, 2, 3)),
            dma((2, 2, 3)), dma((2, 2, 3)),
            dma((2, 2, 2)), dma((2, 2)),
            dma((2, 3)), dma((2, 3)),
            dma((8,)), dma((8,)),
        ],
        compiler_params=pltpu.CompilerParams(
            collective_id=0, has_side_effects=True, vmem_limit_bytes=60 << 20
        ),
    )(
        obs,
        cot,
        cell_basis.reshape(8, 4, 2, 128, 128),
        cycle_basis.reshape(8, 256, 256),
        cell_spectrum.reshape(1, 128),
        cycle_spectrum.reshape(1, 256),
        noise_var,
    )
    return pl.pallas_call(
        hand_over,
        out_shape=(
            jax.ShapeDtypeStruct((256, 128), BF16),
            jax.ShapeDtypeStruct((32, 256), F32),
        ),
        in_specs=[vmem] * 2,
        out_specs=(vmem, vmem),
    )(coefficients, basis_grad)


def solution(mesh):
    in_specs = (
        P("narrow", "wide"),
        P("narrow", "wide"),
        P(None, "wide"),
        P(None, "narrow"),
        P("wide"),
        P("narrow"),
        P(),
    )
    out_specs = (P("narrow", "wide"), P("wide", "narrow"))
    return jax.shard_map(
        on_device, mesh=mesh, in_specs=in_specs, out_specs=out_specs, check_vma=False
    )
```
